32 devices in a mesh: section: 4 (over z), head: 2 (over y), key: 4 (over x, core).
Axes of the slice: x: 2, y: 2, z: 4, core: 2. Of those that a mesh axis runs over, the one named last changes fastest.
Arguments:
- queries: bfloat16 [4, 256, 3072], P('section', None, 'head'), may hold values from -1024 to 1024
- attn_grad: bfloat16 [4, 256, 3072], P('section', None, 'head'), may hold values from -192 to 192
- query_weight: bfloat16 [4, 3072, 3072], P('section', None, 'head'), may hold values from -0.109375 to 0.109375
- key_codes: int32 [4096, 1024], P('key', 'head'), may hold values from -127 to 127
- key_exps: int32 [64, 8], P('key', 'head'), may hold values from -9 to -6
- value_codes: int32 [4096, 1024], P('key', 'head'), may hold values from -127 to 127
- value_exps: int32 [64, 8], P('key', 'head'), may hold values from -9 to -6
Outputs:
- input_grad: bfloat16 [4, 256, 3072], P('section', ('head', 'key'))
- key_grad: float32 [4096, 1024], P(('key', 'section'), 'head')
- value_grad: float32 [4096, 1024], P(('key', 'section'), 'head')
The draws below stay inside these ranges and needn't reach their ends.
All inputs are finite; a program needn't handle non-finite values.
Results may differ from the reference program's by a relative error of at most 0.017.
Values may be sent and summed in bfloat16 or wider, within the bound.
A program may use at most 128 MiB of HBM per device.

```python
import math
import jax
import jax.numpy as jnp
from jax import lax

D = 3072
HQ = 24
KVH = 8
HD = 128
S = 4096
BLK = 64
ROWS = 256
LAYERS = 4
N_HEAD = 2


def key_code_table(key):
    return jax.random.randint(jax.random.fold_in(key, 101), (S, KVH * HD), -127, 128, dtype=jnp.int32)


def key_exponent_table(key):
    return jax.random.randint(jax.random.fold_in(key, 102), (S // BLK, KVH), -9, -5, dtype=jnp.int32)


def draw_key_codes(key, part):
    return key_code_table(key)


def draw_key_exps(key, part):
    return key_exponent_table(key)


def draw_queries(key, part):
    full_shape = (LAYERS, ROWS, HQ * HD)
    row_scale = jnp.exp(jax.random.uniform(jax.random.fold_in(key, 201), (LAYERS, ROWS, 1), minval=math.log(0.25), maxval=math.log(2.5)))
    base_draw = jax.random.normal(jax.random.fold_in(key, 202), full_shape, jnp.float32)
    drawn_draw = 0.3 * row_scale * base_draw
    return jnp.clip(drawn_draw, -1024.0, 1024.0).astype(jnp.bfloat16)


def with_ends(entries, rng, least, top_value):
    longest = entries.shape.index(max(entries.shape))
    spots = []
    for shift in (0, 1):
        where = [jax.random.randint(jax.random.fold_in(rng, axis), (), 0, length) for axis, length in enumerate(entries.shape)]
        where[longest] = (where[longest] + shift) % entries.shape[longest]
        spots.append(tuple(where))
    return entries.at[spots[0]].set(least).at[spots[1]].set(top_value)


def block_levels(stream_key, dims, shards, smallest, high):
    factor_of = 1.0
    for axis_at, blocks in shards:
        heights = jax.random.uniform(jax.random.fold_in(jax.random.fold_in(stream_key, 6), axis_at), (blocks,), jnp.float32, smallest / len(shards), high / len(shards))
        factor_of = factor_of * jnp.repeat(jnp.exp(heights), dims[axis_at] // blocks).reshape((-1,) + (1,) * (len(dims) - 1 - axis_at))
    return factor_of


def bell_draw(stream_key, dims, spread, bound, cuts=(), kind=jnp.bfloat16):
    values = jax.random.normal(stream_key, dims, jnp.float32) * spread
    if len(cuts) > 0:
        values = block_levels(stream_key, dims, cuts, -0.22, 0.18) * values
    return jnp.clip(values, min=-bound, max=bound).astype(kind)


def setup_inputs(seed: int = 0) -> dict:
    seeds = jax.random.split(jax.random.key(seed), 8)
    return {
        "queries": draw_queries(jax.random.fold_in(seeds[7], 71), 0),
        "attn_grad": bell_draw(seeds[1], (LAYERS, ROWS, HQ * HD), 32.0, 192.0, ((0, 4), (2, 2))),
        "query_weight": bell_draw(seeds[2], (LAYERS, D, HQ * HD), D ** -0.5, 0.109375, ((0, 4), (2, 2))),
        "key_codes": draw_key_codes(jax.random.fold_in(seeds[7], 71), 0),
        "key_exps": draw_key_exps(jax.random.fold_in(seeds[7], 71), 0),
        "value_codes": with_ends(jax.random.randint(seeds[5], (S, KVH * HD), -127, 128), jax.random.fold_in(seeds[5], 1), -127, 127).astype(jnp.int32),
        "value_exps": with_ends(jax.random.randint(seeds[6], (S // BLK, KVH), -9, -5), jax.random.fold_in(seeds[6], 1), -9, (-5) - 1).astype(jnp.int32),
    }


def dequantize(code_array, exponents):
    factor = jnp.exp2(exponents.astype(jnp.float32))
    factor = jnp.repeat(factor, BLK, axis=0)
    shaped = code_array.astype(jnp.float32).reshape(S, KVH, HD)
    return (shaped * factor[:, :, None]).astype(jnp.bfloat16)


def per_head(head_args):
    query_head, grad_head, key_head, value_head = head_args
    query_f = query_head.astype(jnp.float32)
    grad_f = grad_head.astype(jnp.float32)
    key_f = key_head.astype(jnp.float32)
    value_f = value_head.astype(jnp.float32)
    score_scale = HD ** -0.5
    scores = jnp.einsum('rgd,sd->grs', query_f, key_f) * score_scale
    row_max = jnp.max(scores, axis=-1, keepdims=True)
    shifted = jnp.exp(scores - row_max)
    probs = shifted / jnp.sum(shifted, axis=-1, keepdims=True)
    grad_probs = jnp.einsum('rgd,sd->grs', grad_f, value_f)
    row_delta = jnp.sum(probs * grad_probs, axis=-1, keepdims=True)
    grad_scores = probs * (grad_probs - row_delta)
    probs_low = lax.optimization_barrier(probs.astype(jnp.bfloat16)).astype(jnp.float32)
    grads_low = lax.optimization_barrier(grad_scores.astype(jnp.bfloat16)).astype(jnp.float32)
    key_part = jnp.einsum('grs,rgd->sd', grads_low, query_f) * score_scale
    value_part = jnp.einsum('grs,rgd->sd', probs_low, grad_f)
    query_part = jnp.einsum('grs,sd->rgd', grads_low, key_f) * score_scale
    return key_part, value_part, query_part


def reference(queries, attn_grad, query_weight, key_codes, key_exps, value_codes, value_exps):
    key_vals = dequantize(key_codes, key_exps).transpose(1, 0, 2)
    value_vals = dequantize(value_codes, value_exps).transpose(1, 0, 2)
    group_size = HQ // KVH
    head_cols = HQ // N_HEAD * HD

    def layer_step(carry_sums, inputs):
        key_sum, value_sum = carry_sums
        query_rows, grad_rows, weight = inputs
        query_heads = query_rows.reshape(ROWS, KVH, group_size, HD).transpose(1, 0, 2, 3)
        grad_heads = grad_rows.reshape(ROWS, KVH, group_size, HD).transpose(1, 0, 2, 3)
        key_part, value_part, query_part = lax.map(per_head, (query_heads, grad_heads, key_vals, value_vals))
        query_grad = query_part.transpose(1, 0, 2, 3).reshape(ROWS, HQ * HD).astype(jnp.bfloat16)
        query_groups = lax.optimization_barrier(query_grad).astype(jnp.float32).reshape(ROWS, N_HEAD, head_cols)
        weight_groups = weight.astype(jnp.float32).reshape(D, N_HEAD, head_cols)
        partial_value = jnp.einsum('rgc,dgc->grd', query_groups, weight_groups)
        partial_value = lax.optimization_barrier(partial_value.astype(jnp.bfloat16)).astype(jnp.float32)
        input_grad = jnp.sum(partial_value, axis=0).astype(jnp.bfloat16)
        return (key_sum + key_part, value_sum + value_part), input_grad

    zero_sums = jnp.zeros((KVH, S, HD), jnp.float32)
    final_sums, input_grad = lax.scan(layer_step, (zero_sums, zero_sums), (queries, attn_grad, query_weight))
    key_grad = final_sums[0].transpose(1, 0, 2).reshape(S, KVH * HD)
    value_grad = final_sums[1].transpose(1, 0, 2).reshape(S, KVH * HD)
    return input_grad, key_grad, value_grad
```

```python
import functools

import jax
import jax.numpy as jnp
from jax import lax
from jax.experimental import pallas as pl
from jax.experimental.pallas import tpu as pltpu
from jax.sharding import PartitionSpec as P

HD = 128
LOG2E = 1.4426950408889634
MESH = pl.DeviceIdType.MESH
F32 = jnp.float32
BF16 = jnp.bfloat16
NT = (((1,), (1,)), ((), ()))
NN = (((1,), (0,)), ((), ()))
TN = (((0,), (0,)), ((), ()))


def dot(a, b, dims):
    return lax.dot_general(a, b, dims, preferred_element_type=F32)


def kernel(
    n_sec, n_head, n_key,
    q_hbm, do_hbm, w_hbm, kc_hbm, ke, vc_hbm, ve,
    in_out, key_out, value_out,
    q_v, do_v, w_v, kc, vc, kd, vd, qs, dos, e_buf, gp_buf,
    blk, st, dq_t, dqb, dqr, qlow, pin, pin_r,
    part, rec_r, rec_l, own,
    load_sem, st_ss, st_rs, dq_ss, dq_rs, in_ss, in_rs, sec_ss, r_rs, l_rs,
):
    sec = lax.axis_index("section")
    head = lax.axis_index("head")
    key = lax.axis_index("key")
    kvl, _, rows_c, _ = kd.shape
    group_rows = qs.shape[1]
    rows = q_v.shape[0]
    group = group_rows // rows
    blk_rows = kc.shape[0] // ke.shape[0]
    block_out = in_out.shape[0]
    scale = HD ** -0.5
    c0 = scale * LOG2E

    barrier = pltpu.get_barrier_semaphore()
    for d in range(1, n_key):
        pl.semaphore_signal(
            barrier, inc=1, device_id={"key": lax.rem(key + d, n_key)}, device_id_type=MESH
        )
    for d in range(1, n_head):
        pl.semaphore_signal(
            barrier, inc=1, device_id={"head": lax.rem(head + d, n_head)}, device_id_type=MESH
        )

    @pl.when(sec > 0)
    def _():
        pl.semaphore_signal(barrier, inc=1, device_id={"section": sec - 1}, device_id_type=MESH)

    @pl.when(sec < n_sec - 1)
    def _():
        pl.semaphore_signal(barrier, inc=1, device_id={"section": sec + 1}, device_id_type=MESH)

    loads = [
        pltpu.make_async_copy(src, dst, load_sem.at[i])
        for i, (src, dst) in enumerate(
            ((kc_hbm, kc), (q_hbm, q_v), (vc_hbm, vc), (do_hbm, do_v), (w_hbm, w_v))
        )
    ]
    for copy in loads:
        copy.start()

    def st_copy(d, g):
        return pltpu.make_async_remote_copy(
            src_ref=st.at[0, g], dst_ref=st.at[d, g],
            send_sem=st_ss.at[d, g], recv_sem=st_rs.at[d, g],
            device_id={"key": lax.rem(key + d, n_key)}, device_id_type=MESH,
        )

    def dq_copy(d, g):
        to = lax.rem(key + d, n_key)
        return pltpu.make_async_remote_copy(
            src_ref=dqb.at[g, to], dst_ref=dqr.at[d - 1, g],
            send_sem=dq_ss.at[d, g], recv_sem=dq_rs.at[d, g],
            device_id={"key": to}, device_id_type=MESH,
        )

    def in_copy(d):
        to = lax.rem(head + d, n_head)
        return pltpu.make_async_remote_copy(
            src_ref=pin.at[to], dst_ref=pin_r.at[d - 1],
            send_sem=in_ss.at[d], recv_sem=in_rs.at[d],
            device_id={"head": to}, device_id_type=MESH,
        )

    def right_copy(c, g):
        return pltpu.make_async_remote_copy(
            src_ref=part.at[c, g], dst_ref=rec_r.at[c, g],
            send_sem=sec_ss.at[c, g], recv_sem=r_rs.at[c, g],
            device_id={"section": jnp.minimum(sec + 1, n_sec - 1)}, device_id_type=MESH,
        )

    def left_copy(c, g):
        return pltpu.make_async_remote_copy(
            src_ref=part.at[c, g], dst_ref=rec_l.at[c, g],
            send_sem=sec_ss.at[c, g], recv_sem=l_rs.at[c, g],
            device_id={"section": jnp.maximum(sec - 1, 0)}, device_id_type=MESH,
        )

    def dequantize(codes, exps, out, g):
        for b in range(exps.shape[0]):
            first = b * blk_rows
            factor = lax.shift_left(jnp.int32(1), exps[b, g] + 16).astype(F32) * (2.0 ** -16)
            block = codes[first : first + blk_rows, g * HD : (g + 1) * HD].astype(F32) * factor
            at = first % rows_c
            out[g, first // rows_c, at : at + blk_rows, :] = block.astype(BF16)

    def stack_heads(src, out, g):
        for h in range(group):
            col = (g * group + h) * HD
            out[g, h * rows : (h + 1) * rows, :] = src[:, col : col + HD]

    def pass_one(g):
        slot = g % 2
        dequantize(kc, ke, kd, g)
        stack_heads(q_v, qs, g)
        if g == 0:
            loads[2].wait()
            loads[3].wait()
        dequantize(vc, ve, vd, g)
        stack_heads(do_v, dos, g)

        def step(c, carry):
            s = dot(kd[g, c], qs[g], NT)
            top = jnp.max(s, axis=0, keepdims=True)
            e = jnp.exp2((s - top) * c0)
            gp = dot(vd[g, c], dos[g], NT)
            e_buf[slot, c] = e
            gp_buf[slot, c] = gp
            blk[slot, c, 0:1, :] = top
            blk[slot, c, 1:2, :] = jnp.sum(e, axis=0, keepdims=True)
            blk[slot, c, 2:3, :] = jnp.sum(e * gp, axis=0, keepdims=True)
            return carry

        lax.fori_loop(0, n_sec, step, 0)
        tops = blk[slot, :, 0:1, :]
        top = jnp.max(tops, axis=0)
        weight = jnp.exp2((tops - top[None]) * c0)
        st[0, g, 0:1, :] = top
        st[0, g, 1:2, :] = jnp.sum(blk[slot, :, 1:2, :] * weight, axis=0)
        st[0, g, 2:3, :] = jnp.sum(blk[slot, :, 2:3, :] * weight, axis=0)
        st[0, g, 3:8, :] = jnp.zeros((5, group_rows), F32)
        if g == 0:
            beside = jnp.where(sec > 0, 1, 0) + jnp.where(sec < n_sec - 1, 1, 0)
            pl.semaphore_wait(barrier, n_key - 1 + n_head - 1 + beside)

        for d in range(1, n_key):
            st_copy(d, g).start()

    def pass_two(g):
        slot = g % 2
        for d in range(1, n_key):
            st_copy(d, g).wait_recv()
        tops = [st[d, g, 0:1, :] for d in range(n_key)]
        top = functools.reduce(jnp.maximum, tops)
        weights = [jnp.exp2((t - top) * c0) for t in tops]
        total = sum(st[d, g, 1:2, :] * weights[d] for d in range(n_key))
        inverse = 1.0 / total
        delta = sum(st[d, g, 2:3, :] * weights[d] for d in range(n_key)) * inverse
        dq_t[...] = jnp.zeros_like(dq_t)

        def step(t, carry):
            c = jnp.where(sec < n_sec // 2, n_sec - 1 - t, t)
            alpha = jnp.exp2((blk[slot, c, 0:1, :] - top) * c0) * inverse
            p = e_buf[slot, c] * alpha
            ds = (p * (gp_buf[slot, c] - delta)).astype(BF16)
            value_part = dot(p.astype(BF16), dos[g], NN)
            key_part = dot(ds, qs[g], NN) * scale
            dq_t[...] += dot(kd[g, c], ds, TN)

            @pl.when(c == sec)
            def _():
                own[g, 0] = key_part
                own[g, 1] = value_part

            @pl.when(c != sec)
            def _():
                part[c, g, 0] = key_part.astype(BF16)
                part[c, g, 1] = value_part.astype(BF16)

            @pl.when(jnp.logical_and(sec == 0, c > 0))
            def _():
                right_copy(c, g).start()

            @pl.when(jnp.logical_and(sec == n_sec - 1, c < n_sec - 1))
            def _():
                left_copy(c, g).start()

            return carry

        lax.fori_loop(0, n_sec, step, 0)
        dq = (jnp.transpose(dq_t[...]) * scale).astype(BF16)
        for k in range(n_key):
            for hh in range(n_head):
                for h in range(group):
                    first = h * rows + (hh * n_key + k) * block_out
                    dqb[g, k, hh * block_out : (hh + 1) * block_out, h * HD : (h + 1) * HD] = dq[
                        first : first + block_out
                    ]
        for d in range(1, n_key):
            dq_copy(d, g).start()

    def forward(g):
        def step(t, carry):
            right = n_sec - 1 - t

            @pl.when(jnp.logical_and(right > sec, sec > 0))
            def _():
                right_copy(right, g).wait_recv()
                part[right, g] = (
                    part[right, g].astype(F32) + rec_r[right, g].astype(F32)
                ).astype(BF16)
                right_copy(right, g).start()

            @pl.when(jnp.logical_and(t < sec, sec < n_sec - 1))
            def _():
                left_copy(t, g).wait_recv()
                part[t, g] = (part[t, g].astype(F32) + rec_l[t, g].astype(F32)).astype(BF16)
                left_copy(t, g).start()

            return carry

        lax.fori_loop(0, n_sec, step, 0)

    def finish(g):
        @pl.when(sec > 0)
        def _():
            right_copy(sec, g).wait_recv()
            own[g] += rec_r[sec, g].astype(F32)

        @pl.when(sec < n_sec - 1)
        def _():
            left_copy(sec, g).wait_recv()
            own[g] += rec_l[sec, g].astype(F32)

        key_out[:, g * HD : (g + 1) * HD] = own[g, 0]
        value_out[:, g * HD : (g + 1) * HD] = own[g, 1]

    loads[0].wait()
    loads[1].wait()
    pass_one(0)
    for g in range(1, kvl):
        pass_one(g)
        pass_two(g - 1)
    pass_two(kvl - 1)
    forward(0)

    width = group * HD
    for g in range(kvl):
        for d in range(1, n_key):
            dq_copy(d, g).wait_recv()
        total = dqb[g, key].astype(F32)
        for d in range(1, n_key):
            total = total + dqr[d - 1, g].astype(F32)
        qlow[:, g * width : (g + 1) * width] = total.astype(BF16)
    loads[4].wait()
    wide = w_v.shape[0]
    tile = 512

    def columns(i, carry):
        first = pl.multiple_of(i * tile, tile)
        product = dot(qlow[...], w_v[pl.ds(first, tile), :], NT).astype(BF16)
        for hh in range(n_head):
            pin[hh, :, pl.ds(first, tile)] = product[hh * block_out : (hh + 1) * block_out]
        return carry

    lax.fori_loop(0, wide // tile, columns, 0)
    for d in range(1, n_head):
        in_copy(d).start()

    finish(0)
    for g in range(1, kvl):
        forward(g)
        finish(g)

    for d in range(1, n_head):
        in_copy(d).wait_recv()
    total = pin[head].astype(F32)
    for d in range(1, n_head):
        total = total + pin_r[d - 1].astype(F32)
    in_out[...] = total.astype(BF16)

    for g in range(kvl):
        for d in range(1, n_key):
            st_copy(d, g).wait_send()
            dq_copy(d, g).wait_send()

        def drain(c, carry, g=g):
            @pl.when(c > sec)
            def _():
                right_copy(c, g).wait_send()

            @pl.when(c < sec)
            def _():
                left_copy(c, g).wait_send()

            return carry

        lax.fori_loop(0, n_sec, drain, 0)
    for d in range(1, n_head):
        in_copy(d).wait_send()


def body(n_sec, n_head, n_key, queries, attn_grad, query_weight, kc, ke, vc, ve):
    rows, cols = queries.shape[1:]
    wide = query_weight.shape[1]
    positions, kv_cols = kc.shape
    kvl = kv_cols // HD
    group_rows = cols // kv_cols * rows
    rows_c = positions // n_sec
    block_out = rows // (n_head * n_key)
    group_cols = cols // kvl
    vmem = pltpu.VMEM
    dma = pltpu.SemaphoreType.DMA
    anywhere = pl.BlockSpec(memory_space=pl.ANY)
    scalars = pl.BlockSpec(memory_space=pltpu.SMEM)
    in_vmem = pl.BlockSpec(memory_space=pltpu.VMEM)
    input_grad, key_grad, value_grad = pl.pallas_call(
        functools.partial(kernel, n_sec, n_head, n_key),
        out_shape=(
            jax.ShapeDtypeStruct((block_out, wide), BF16),
            jax.ShapeDtypeStruct((rows_c, kv_cols), F32),
            jax.ShapeDtypeStruct((rows_c, kv_cols), F32),
        ),
        in_specs=[anywhere, anywhere, anywhere, anywhere, scalars, anywhere, scalars],
        out_specs=(in_vmem, in_vmem, in_vmem),
        scratch_shapes=[
            vmem((rows, cols), BF16),
            vmem((rows, cols), BF16),
            vmem((wide, cols), BF16),
            vmem((positions, kv_cols), jnp.int32),
            vmem((positions, kv_cols), jnp.int32),
            vmem((kvl, n_sec, rows_c, HD), BF16),
            vmem((kvl, n_sec, rows_c, HD), BF16),
            vmem((kvl, group_rows, HD), BF16),
            vmem((kvl, group_rows, HD), BF16),
            vmem((2, n_sec, rows_c, group_rows), F32),
            vmem((2, n_sec, rows_c, group_rows), F32),
            vmem((2, n_sec, 8, group_rows), F32),
            vmem((n_key, kvl, 8, group_rows), F32),
            vmem((HD, group_rows), F32),
            vmem((kvl, n_key, n_head * block_out, group_cols), BF16),
            vmem((n_key - 1, kvl, n_head * block_out, group_cols), BF16),
            vmem((n_head * block_out, cols), BF16),
            vmem((n_head, block_out, wide), BF16),
            vmem((n_head - 1, block_out, wide), BF16),
            vmem((n_sec, kvl, 2, rows_c, HD), BF16),
            vmem((n_sec, kvl, 2, rows_c, HD), BF16),
            vmem((n_sec, kvl, 2, rows_c, HD), BF16),
            vmem((kvl, 2, rows_c, HD), F32),
            dma((5,)),
            dma((n_key, kvl)),
            dma((n_key, kvl)),
            dma((n_key, kvl)),
            dma((n_key, kvl)),
            dma((n_head,)),
            dma((n_head,)),
            dma((n_sec, kvl)),
            dma((n_sec, kvl)),
            dma((n_sec, kvl)),
        ],
        compiler_params=pltpu.CompilerParams(
            collective_id=0, has_side_effects=True, vmem_limit_bytes=58 * 1024 * 1024
        ),
    )(queries[0], attn_grad[0], query_weight[0], kc, ke, vc, ve)
    return input_grad[None], key_grad, value_grad


def solution(mesh):
    shape = mesh.shape
    return jax.shard_map(
        functools.partial(body, shape["section"], shape["head"], shape["key"]),
        mesh=mesh,
        in_specs=(
            P("section", None, "head"),
            P("section", None, "head"),
            P("section", None, "head"),
            P("key", "head"),
            P("key", "head"),
            P("key", "head"),
            P("key", "head"),
        ),
        out_specs=(
            P("section", ("head", "key"), None),
            P(("key", "section"), "head"),
            P(("key", "section"), "head"),
        ),
        check_vma=False,
    )
```

```python
import functools

import jax
import jax.numpy as jnp
from jax import lax
from jax.experimental import pallas as pl
from jax.experimental.pallas import tpu as pltpu
from jax.sharding import PartitionSpec as P

HD = 128
LOG2E = 1.4426950408889634
MESH = pl.DeviceIdType.MESH
F32 = jnp.float32
BF16 = jnp.bfloat16
NT = (((1,), (1,)), ((), ()))
NN = (((1,), (0,)), ((), ()))
TN = (((0,), (0,)), ((), ()))


def dot(a, b, dims):
    return lax.dot_general(a, b, dims, preferred_element_type=F32)


def kernel(
    n_sec, n_head, n_key,
    q_hbm, do_hbm, w_hbm, kc_hbm, ke_hbm, vc_hbm, ve_hbm,
    in_out, key_out, value_out,
    ke, ve, w_v, kc, vc, kd, vd, qs, dos, e_buf, gp_buf,
    blk, st, dq_t, dqb, dqr, qlow, pin, pin_r,
    part, rec_r, rec_l, own,
    exp_sem, code_sem, row_sem, w_sem, st_ss, st_rs, dq_ss, dq_rs, in_ss, in_rs, sec_ss, r_rs, l_rs,
):
    sec = lax.axis_index("section")
    head = lax.axis_index("head")
    key = lax.axis_index("key")
    kvl, _, rows_c, _ = kd.shape
    group_rows = qs.shape[1]
    rows = q_hbm.shape[0]
    group = group_rows // rows
    blk_rows = kc.shape[0] // ke.shape[1]
    block_out = in_out.shape[0]
    scale = HD ** -0.5
    c0 = scale * LOG2E

    barrier = pltpu.get_barrier_semaphore()
    for d in range(1, n_key):
        pl.semaphore_signal(
            barrier, inc=1, device_id={"key": lax.rem(key + d, n_key)}, device_id_type=MESH
        )
    for d in range(1, n_head):
        pl.semaphore_signal(
            barrier, inc=1, device_id={"head": lax.rem(head + d, n_head)}, device_id_type=MESH
        )

    @pl.when(sec > 0)
    def _():
        pl.semaphore_signal(barrier, inc=1, device_id={"section": sec - 1}, device_id_type=MESH)

    @pl.when(sec < n_sec - 1)
    def _():
        pl.semaphore_signal(barrier, inc=1, device_id={"section": sec + 1}, device_id_type=MESH)

    def code_load(i, g):
        src, dst = ((kc_hbm, kc), (vc_hbm, vc))[i]
        cols = pl.ds(g * HD, HD)
        return pltpu.make_async_copy(src.at[:, cols], dst.at[:, cols], code_sem.at[i, g])

    def row_load(i, g, h):
        src, dst = ((q_hbm, qs), (do_hbm, dos))[i]
        return pltpu.make_async_copy(
            src.at[:, pl.ds((g * group + h) * HD, HD)],
            dst.at[g, pl.ds(h * rows, rows)],
            row_sem.at[i, g, h],
        )

    exp_loads = [
        pltpu.make_async_copy(ke_hbm, ke, exp_sem.at[0]),
        pltpu.make_async_copy(ve_hbm, ve, exp_sem.at[1]),
    ]
    w_load = pltpu.make_async_copy(w_hbm, w_v, w_sem)
    for copy in exp_loads:
        copy.start()
    for g in range(kvl):
        for i in range(2):
            code_load(i, g).start()
            for h in range(group):
                row_load(i, g, h).start()

    def st_copy(d, g):
        return pltpu.make_async_remote_copy(
            src_ref=st.at[0, g], dst_ref=st.at[d, g],
            send_sem=st_ss.at[d, g], recv_sem=st_rs.at[d, g],
            device_id={"key": lax.rem(key + d, n_key)}, device_id_type=MESH,
        )

    def dq_copy(d, g):
        to = lax.rem(key + d, n_key)
        return pltpu.make_async_remote_copy(
            src_ref=dqb.at[g, to], dst_ref=dqr.at[d - 1, g],
            send_sem=dq_ss.at[d, g], recv_sem=dq_rs.at[d, g],
            device_id={"key": to}, device_id_type=MESH,
        )

    def in_copy(d):
        to = lax.rem(head + d, n_head)
        return pltpu.make_async_remote_copy(
            src_ref=pin.at[to], dst_ref=pin_r.at[d - 1],
            send_sem=in_ss.at[d], recv_sem=in_rs.at[d],
            device_id={"head": to}, device_id_type=MESH,
        )

    def right_copy(c, g):
        return pltpu.make_async_remote_copy(
            src_ref=part.at[c, g], dst_ref=rec_r.at[c, g],
            send_sem=sec_ss.at[c, g], recv_sem=r_rs.at[c, g],
            device_id={"section": jnp.minimum(sec + 1, n_sec - 1)}, device_id_type=MESH,
        )

    def left_copy(c, g):
        return pltpu.make_async_remote_copy(
            src_ref=part.at[c, g], dst_ref=rec_l.at[c, g],
            send_sem=sec_ss.at[c, g], recv_sem=l_rs.at[c, g],
            device_id={"section": jnp.maximum(sec - 1, 0)}, device_id_type=MESH,
        )

    def dequantize(codes, exps, out, g):
        factors = lax.shift_left(jnp.int32(1), exps[...] + 16).astype(F32) * (2.0 ** -16)
        for b in range(exps.shape[1]):
            first = b * blk_rows
            block = codes[first : first + blk_rows, g * HD : (g + 1) * HD].astype(F32)
            at = first % rows_c
            out[g, first // rows_c, at : at + blk_rows, :] = (
                block * factors[g : g + 1, b : b + 1]
            ).astype(BF16)

    def pass_one(g):
        slot = g % 2
        for i, (codes, exps, out) in enumerate(((kc, ke, kd), (vc, ve, vd))):
            if g == 0:
                exp_loads[i].wait()
            code_load(i, g).wait()
            dequantize(codes, exps, out, g)
            for h in range(group):
                row_load(i, g, h).wait()

        def step(c, carry):
            s = dot(kd[g, c], qs[g], NT)
            top = jnp.max(s, axis=0, keepdims=True)
            e = jnp.exp2((s - top) * c0)
            gp = dot(vd[g, c], dos[g], NT)
            e_buf[slot, c] = e
            gp_buf[slot, c] = gp
            blk[slot, c, 0:1, :] = top
            blk[slot, c, 1:2, :] = jnp.sum(e, axis=0, keepdims=True)
            blk[slot, c, 2:3, :] = jnp.sum(e * gp, axis=0, keepdims=True)
            return carry

        lax.fori_loop(0, n_sec, step, 0)
        tops = blk[slot, :, 0:1, :]
        top = jnp.max(tops, axis=0)
        weight = jnp.exp2((tops - top[None]) * c0)
        st[0, g, 0:1, :] = top
        st[0, g, 1:2, :] = jnp.sum(blk[slot, :, 1:2, :] * weight, axis=0)
        st[0, g, 2:3, :] = jnp.sum(blk[slot, :, 2:3, :] * weight, axis=0)
        st[0, g, 3:8, :] = jnp.zeros((5, group_rows), F32)
        if g == 0:
            beside = jnp.where(sec > 0, 1, 0) + jnp.where(sec < n_sec - 1, 1, 0)
            pl.semaphore_wait(barrier, n_key - 1 + n_head - 1 + beside)
            w_load.start()

        for d in range(1, n_key):
            st_copy(d, g).start()

    def pass_two(g):
        slot = g % 2
        for d in range(1, n_key):
            st_copy(d, g).wait_recv()
        tops = [st[d, g, 0:1, :] for d in range(n_key)]
        top = functools.reduce(jnp.maximum, tops)
        weights = [jnp.exp2((t - top) * c0) for t in tops]
        total = sum(st[d, g, 1:2, :] * weights[d] for d in range(n_key))
        inverse = 1.0 / total
        delta = sum(st[d, g, 2:3, :] * weights[d] for d in range(n_key)) * inverse
        dq_t[...] = jnp.zeros_like(dq_t)

        def step(t, carry):
            c = jnp.where(sec < n_sec // 2, n_sec - 1 - t, t)
            alpha = jnp.exp2((blk[slot, c, 0:1, :] - top) * c0) * inverse
            p = e_buf[slot, c] * alpha
            ds = (p * (gp_buf[slot, c] - delta)).astype(BF16)
            value_part = dot(p.astype(BF16), dos[g], NN)
            key_part = dot(ds, qs[g], NN) * scale
            dq_t[...] += dot(kd[g, c], ds, TN)

            @pl.when(c == sec)
            def _():
                own[g, 0] = key_part
                own[g, 1] = value_part

            @pl.when(c != sec)
            def _():
                part[c, g, 0] = key_part.astype(BF16)
                part[c, g, 1] = value_part.astype(BF16)

            @pl.when(jnp.logical_and(sec == 0, c > 0))
            def _():
                right_copy(c, g).start()

            @pl.when(jnp.logical_and(sec == n_sec - 1, c < n_sec - 1))
            def _():
                left_copy(c, g).start()

            return carry

        lax.fori_loop(0, n_sec, step, 0)
        dq = (jnp.transpose(dq_t[...]) * scale).astype(BF16)
        for k in range(n_key):
            for hh in range(n_head):
                for h in range(group):
                    first = h * rows + (hh * n_key + k) * block_out
                    dqb[g, k, hh * block_out : (hh + 1) * block_out, h * HD : (h + 1) * HD] = dq[
                        first : first + block_out
                    ]
        for d in range(1, n_key):
            dq_copy(d, g).start()

    def relay(stage):
        inner = jnp.logical_and(sec > 0, sec < n_sec - 1)
        right_g, left_g = stage - sec, stage - (n_sec - 1 - sec)
        right_on = jnp.logical_and(inner, jnp.logical_and(right_g >= 0, right_g < kvl))
        left_on = jnp.logical_and(inner, jnp.logical_and(left_g >= 0, left_g < kvl))
        rg, lg = jnp.clip(right_g, 0, kvl - 1), jnp.clip(left_g, 0, kvl - 1)

        def step(t, carry):
            right = n_sec - 1 - t

            @pl.when(jnp.logical_and(right > sec, right_on))
            def _():
                right_copy(right, rg).wait_recv()
                part[right, rg] = (
                    part[right, rg].astype(F32) + rec_r[right, rg].astype(F32)
                ).astype(BF16)
                right_copy(right, rg).start()

            @pl.when(jnp.logical_and(t < sec, left_on))
            def _():
                left_copy(t, lg).wait_recv()
                part[t, lg] = (part[t, lg].astype(F32) + rec_l[t, lg].astype(F32)).astype(BF16)
                left_copy(t, lg).start()

            return carry

        lax.fori_loop(0, n_sec, step, 0)

    def finish(g):
        @pl.when(sec > 0)
        def _():
            right_copy(sec, g).wait_recv()
            own[g] += rec_r[sec, g].astype(F32)

        @pl.when(sec < n_sec - 1)
        def _():
            left_copy(sec, g).wait_recv()
            own[g] += rec_l[sec, g].astype(F32)

        key_out[:, g * HD : (g + 1) * HD] = own[g, 0]
        value_out[:, g * HD : (g + 1) * HD] = own[g, 1]

    pass_one(0)
    for g in range(1, kvl):
        pass_one(g)
        pass_two(g - 1)
        if g > 1:
            relay(g - 1)
    pass_two(kvl - 1)
    relay(kvl - 1)

    width = group * HD
    for g in range(kvl):
        for d in range(1, n_key):
            dq_copy(d, g).wait_recv()
        total = dqb[g, key].astype(F32)
        for d in range(1, n_key):
            total = total + dqr[d - 1, g].astype(F32)
        qlow[:, g * width : (g + 1) * width] = total.astype(BF16)
    w_load.wait()
    wide = w_v.shape[0]
    tile = 512

    def columns(i, carry):
        first = pl.multiple_of(i * tile, tile)
        product = dot(qlow[...], w_v[pl.ds(first, tile), :], NT).astype(BF16)
        for hh in range(n_head):
            pin[hh, :, pl.ds(first, tile)] = product[hh * block_out : (hh + 1) * block_out]
        return carry

    half = wide // tile // 2
    lax.fori_loop(0, half, columns, 0)
    relay(kvl)
    lax.fori_loop(half, wide // tile, columns, 0)
    for d in range(1, n_head):
        in_copy(d).start()
    for stage in range(kvl + 1, kvl + n_sec - 2):
        relay(stage)
    for g in range(kvl):
        finish(g)

    for d in range(1, n_head):
        in_copy(d).wait_recv()
    total = pin[head].astype(F32)
    for d in range(1, n_head):
        total = total + pin_r[d - 1].astype(F32)
    in_out[...] = total.astype(BF16)

    for g in range(kvl):
        for d in range(1, n_key):
            st_copy(d, g).wait_send()
            dq_copy(d, g).wait_send()

        def drain(c, carry, g=g):
            @pl.when(c > sec)
            def _():
                right_copy(c, g).wait_send()

            @pl.when(c < sec)
            def _():
                left_copy(c, g).wait_send()

            return carry

        lax.fori_loop(0, n_sec, drain, 0)
    for d in range(1, n_head):
        in_copy(d).wait_send()


def hand_out(a, b, c, a_out, b_out, c_out, sem):
    copies = [
        pltpu.make_async_copy(src, dst, sem.at[i])
        for i, (src, dst) in enumerate(((a, a_out), (b, b_out), (c, c_out)))
    ]
    for copy in copies:
        copy.start()
    for copy in copies:
        copy.wait()


def body(n_sec, n_head, n_key, queries, attn_grad, query_weight, kc, ke, vc, ve):
    rows, cols = queries.shape[1:]
    wide = query_weight.shape[1]
    positions, kv_cols = kc.shape
    kvl = kv_cols // HD
    group_rows = cols // kv_cols * rows
    rows_c = positions // n_sec
    block_out = rows // (n_head * n_key)
    group_cols = cols // kvl
    vmem = pltpu.VMEM
    dma = pltpu.SemaphoreType.DMA
    anywhere = pl.BlockSpec(memory_space=pl.ANY)
    in_vmem = pl.BlockSpec(memory_space=pltpu.VMEM)
    results = pl.pallas_call(
        functools.partial(kernel, n_sec, n_head, n_key),
        out_shape=(
            jax.ShapeDtypeStruct((block_out, wide), BF16),
            jax.ShapeDtypeStruct((rows_c, kv_cols), F32),
            jax.ShapeDtypeStruct((rows_c, kv_cols), F32),
        ),
        in_specs=[anywhere] * 7,
        out_specs=(in_vmem, in_vmem, in_vmem),
        scratch_shapes=[
            vmem(ke.T.shape, jnp.int32),
            vmem(ve.T.shape, jnp.int32),
            vmem((wide, cols), BF16),
            vmem((positions, kv_cols), jnp.int32),
            vmem((positions, kv_cols), jnp.int32),
            vmem((kvl, n_sec, rows_c, HD), BF16),
            vmem((kvl, n_sec, rows_c, HD), BF16),
            vmem((kvl, group_rows, HD), BF16),
            vmem((kvl, group_rows, HD), BF16),
            vmem((2, n_sec, rows_c, group_rows), F32),
            vmem((2, n_sec, rows_c, group_rows), F32),
            vmem((2, n_sec, 8, group_rows), F32),
            vmem((n_key, kvl, 8, group_rows), F32),
            vmem((HD, group_rows), F32),
            vmem((kvl, n_key, n_head * block_out, group_cols), BF16),
            vmem((n_key - 1, kvl, n_head * block_out, group_cols), BF16),
            vmem((n_head * block_out, cols), BF16),
            vmem((n_head, block_out, wide), BF16),
            vmem((n_head - 1, block_out, wide), BF16),
            vmem((n_sec, kvl, 2, rows_c, HD), BF16),
            vmem((n_sec, kvl, 2, rows_c, HD), BF16),
            vmem((n_sec, kvl, 2, rows_c, HD), BF16),
            vmem((kvl, 2, rows_c, HD), F32),
            dma((2,)),
            dma((2, kvl)),
            dma((2, kvl, cols // kv_cols)),
            dma,
            dma((n_key, kvl)),
            dma((n_key, kvl)),
            dma((n_key, kvl)),
            dma((n_key, kvl)),
            dma((n_head,)),
            dma((n_head,)),
            dma((n_sec, kvl)),
            dma((n_sec, kvl)),
            dma((n_sec, kvl)),
        ],
        compiler_params=pltpu.CompilerParams(
            collective_id=0, has_side_effects=True, vmem_limit_bytes=58 * 1024 * 1024
        ),
    )(queries[0], attn_grad[0], query_weight[0], kc, ke.T, vc, ve.T)
    input_grad, key_grad, value_grad = pl.pallas_call(
        hand_out,
        out_shape=tuple(jax.ShapeDtypeStruct(r.shape, r.dtype) for r in results),
        in_specs=[anywhere] * 3,
        out_specs=(anywhere,) * 3,
        scratch_shapes=[dma((3,))],
        compiler_params=pltpu.CompilerParams(vmem_limit_bytes=62 * 1024 * 1024),
    )(*results)
    return input_grad[None], key_grad, value_grad


def solution(mesh):
    shape = mesh.shape
    return jax.shard_map(
        functools.partial(body, shape["section"], shape["head"], shape["key"]),
        mesh=mesh,
        in_specs=(
            P("section", None, "head"),
            P("section", None, "head"),
            P("section", None, "head"),
            P("key", "head"),
            P("key", "head"),
            P("key", "head"),
            P("key", "head"),
        ),
        out_specs=(
            P("section", ("head", "key"), None),
            P(("key", "section"), "head"),
            P(("key", "section"), "head"),
        ),
        check_vma=False,
    )
```

```python
import functools

import jax
import jax.numpy as jnp
from jax import lax
from jax.experimental import pallas as pl
from jax.experimental.pallas import tpu as pltpu
from jax.sharding import PartitionSpec as P

HD = 128
LOG2E = 1.4426950408889634
MESH = pl.DeviceIdType.MESH
F32 = jnp.float32
BF16 = jnp.bfloat16
NT = (((1,), (1,)), ((), ()))
NN = (((1,), (0,)), ((), ()))
TN = (((0,), (0,)), ((), ()))


def dot(a, b, dims):
    return lax.dot_general(a, b, dims, preferred_element_type=F32)


def kernel(
    n_sec, n_head, n_key,
    q_hbm, do_hbm, w_hbm, kc_hbm, ke_hbm, vc_hbm, ve_hbm,
    in_out, key_out, value_out,
    ke, ve, w_v, kc, vc, kd, vd, qs, dos, e_buf, gp_buf,
    blk, st, dq_t, dqb, dqr, qlow, pin, pin_r,
    part, rec_r, rec_l, own,
    exp_sem, code_sem, row_sem, w_sem, st_ss, st_rs, dq_ss, dq_rs, in_ss, in_rs, sec_ss, r_rs, l_rs,
):
    sec = lax.axis_index("section")
    head = lax.axis_index("head")
    key = lax.axis_index("key")
    kvl, _, rows_c, _ = kd.shape
    group_rows = qs.shape[1]
    rows = q_hbm.shape[0]
    group = group_rows // rows
    blk_rows = kc.shape[0] // ke.shape[1]
    block_out = in_out.shape[0]
    scale = HD ** -0.5
    c0 = scale * LOG2E

    barrier = pltpu.get_barrier_semaphore()
    for d in range(1, n_key):
        pl.semaphore_signal(
            barrier, inc=1, device_id={"key": lax.rem(key + d, n_key)}, device_id_type=MESH
        )
    for d in range(1, n_head):
        pl.semaphore_signal(
            barrier, inc=1, device_id={"head": lax.rem(head + d, n_head)}, device_id_type=MESH
        )

    @pl.when(sec > 0)
    def _():
        pl.semaphore_signal(barrier, inc=1, device_id={"section": sec - 1}, device_id_type=MESH)

    @pl.when(sec < n_sec - 1)
    def _():
        pl.semaphore_signal(barrier, inc=1, device_id={"section": sec + 1}, device_id_type=MESH)

    def code_load(i, g):
        src, dst = ((kc_hbm, kc), (vc_hbm, vc))[i]
        cols = pl.ds(g * HD, HD)
        return pltpu.make_async_copy(src.at[:, cols], dst.at[:, cols], code_sem.at[i, g])

    def row_load(i, g, h):
        src, dst = ((q_hbm, qs), (do_hbm, dos))[i]
        return pltpu.make_async_copy(
            src.at[:, pl.ds((g * group + h) * HD, HD)],
            dst.at[g, pl.ds(h * rows, rows)],
            row_sem.at[i, g, h],
        )

    exp_loads = [
        pltpu.make_async_copy(ke_hbm, ke, exp_sem.at[0]),
        pltpu.make_async_copy(ve_hbm, ve, exp_sem.at[1]),
    ]
    w_load = pltpu.make_async_copy(w_hbm, w_v, w_sem)
    for copy in exp_loads:
        copy.start()
    for g in range(kvl):
        for i in range(2):
            code_load(i, g).start()
            for h in range(group):
                row_load(i, g, h).start()

    def st_copy(d, g):
        return pltpu.make_async_remote_copy(
            src_ref=st.at[0, g], dst_ref=st.at[d, g],
            send_sem=st_ss.at[d, g], recv_sem=st_rs.at[d, g],
            device_id={"key": lax.rem(key + d, n_key)}, device_id_type=MESH,
        )

    def dq_copy(d, g):
        to = lax.rem(key + d, n_key)
        return pltpu.make_async_remote_copy(
            src_ref=dqb.at[g, to], dst_ref=dqr.at[d - 1, g],
            send_sem=dq_ss.at[d, g], recv_sem=dq_rs.at[d, g],
            device_id={"key": to}, device_id_type=MESH,
        )

    def in_copy(d):
        to = lax.rem(head + d, n_head)
        return pltpu.make_async_remote_copy(
            src_ref=pin.at[to], dst_ref=pin_r.at[d - 1],
            send_sem=in_ss.at[d], recv_sem=in_rs.at[d],
            device_id={"head": to}, device_id_type=MESH,
        )

    def right_copy(c, g):
        return pltpu.make_async_remote_copy(
            src_ref=part.at[c, g], dst_ref=rec_r.at[c, g],
            send_sem=sec_ss.at[c, g], recv_sem=r_rs.at[c, g],
            device_id={"section": jnp.minimum(sec + 1, n_sec - 1)}, device_id_type=MESH,
        )

    def left_copy(c, g):
        return pltpu.make_async_remote_copy(
            src_ref=part.at[c, g], dst_ref=rec_l.at[c, g],
            send_sem=sec_ss.at[c, g], recv_sem=l_rs.at[c, g],
            device_id={"section": jnp.maximum(sec - 1, 0)}, device_id_type=MESH,
        )

    def dequantize(codes, exps, out, g):
        factors = lax.shift_left(jnp.int32(1), exps[...] + 16).astype(F32) * (2.0 ** -16)
        for b in range(exps.shape[1]):
            first = b * blk_rows
            block = codes[first : first + blk_rows, g * HD : (g + 1) * HD].astype(F32)
            at = first % rows_c
            out[g, first // rows_c, at : at + blk_rows, :] = (
                block * factors[g : g + 1, b : b + 1]
            ).astype(BF16)

    def unpack(g):
        for i, (codes, exps, out) in enumerate(((kc, ke, kd), (vc, ve, vd))):
            if g == 0:
                exp_loads[i].wait()
            code_load(i, g).wait()
            dequantize(codes, exps, out, g)
            for h in range(group):
                row_load(i, g, h).wait()

    def pass_one(g):
        slot = g % 2

        def step(c, carry):
            keys, values = kd[g, c], vd[g, c]
            for h in range(group):
                cols = slice(h * rows, (h + 1) * rows)
                s = dot(keys, qs[g, cols], NT)
                gp = dot(values, dos[g, cols], NT)
                top = jnp.max(s, axis=0, keepdims=True)
                e = jnp.exp2((s - top) * c0)
                e_buf[slot, c, :, cols] = e
                gp_buf[slot, c, :, cols] = gp
                blk[slot, c, 0:1, cols] = top
                blk[slot, c, 1:2, cols] = jnp.sum(e, axis=0, keepdims=True)
                blk[slot, c, 2:3, cols] = jnp.sum(e * gp, axis=0, keepdims=True)
            return carry

        lax.fori_loop(0, n_sec, step, 0)
        tops = blk[slot, :, 0:1, :]
        top = jnp.max(tops, axis=0)
        weight = jnp.exp2((tops - top[None]) * c0)
        st[0, g, 0:1, :] = top
        st[0, g, 1:2, :] = jnp.sum(blk[slot, :, 1:2, :] * weight, axis=0)
        st[0, g, 2:3, :] = jnp.sum(blk[slot, :, 2:3, :] * weight, axis=0)
        st[0, g, 3:8, :] = jnp.zeros((5, group_rows), F32)
        if g == 0:
            beside = jnp.where(sec > 0, 1, 0) + jnp.where(sec < n_sec - 1, 1, 0)
            pl.semaphore_wait(barrier, n_key - 1 + n_head - 1 + beside)
            w_load.start()

        for d in range(1, n_key):
            st_copy(d, g).start()

    def pass_two(g):
        slot = g % 2
        for d in range(1, n_key):
            st_copy(d, g).wait_recv()
        tops = [st[d, g, 0:1, :] for d in range(n_key)]
        top = functools.reduce(jnp.maximum, tops)
        weights = [jnp.exp2((t - top) * c0) for t in tops]
        total = sum(st[d, g, 1:2, :] * weights[d] for d in range(n_key))
        inverse = 1.0 / total
        delta = sum(st[d, g, 2:3, :] * weights[d] for d in range(n_key)) * inverse
        dq_t[...] = jnp.zeros_like(dq_t)

        def step(t, carry):
            c = jnp.where(sec < n_sec // 2, n_sec - 1 - t, t)
            alpha = jnp.exp2((blk[slot, c, 0:1, :] - top) * c0) * inverse
            p = e_buf[slot, c] * alpha
            ds = (p * (gp_buf[slot, c] - delta)).astype(BF16)
            value_part = dot(p.astype(BF16), dos[g], NN)
            key_part = dot(ds, qs[g], NN) * scale
            dq_t[...] += dot(kd[g, c], ds, TN)

            @pl.when(c == sec)
            def _():
                own[g, 0] = key_part
                own[g, 1] = value_part

            @pl.when(c != sec)
            def _():
                part[c, g, 0] = key_part.astype(BF16)
                part[c, g, 1] = value_part.astype(BF16)

            @pl.when(jnp.logical_and(sec == 0, c > 0))
            def _():
                right_copy(c, g).start()

            @pl.when(jnp.logical_and(sec == n_sec - 1, c < n_sec - 1))
            def _():
                left_copy(c, g).start()

            return carry

        lax.fori_loop(0, n_sec, step, 0)
        dq = (jnp.transpose(dq_t[...]) * scale).astype(BF16)
        for k in range(n_key):
            for hh in range(n_head):
                for h in range(group):
                    first = h * rows + (hh * n_key + k) * block_out
                    dqb[g, k, hh * block_out : (hh + 1) * block_out, h * HD : (h + 1) * HD] = dq[
                        first : first + block_out
                    ]
        for d in range(1, n_key):
            dq_copy(d, g).start()

    def relay(stage):
        inner = jnp.logical_and(sec > 0, sec < n_sec - 1)
        right_g, left_g = stage - sec, stage - (n_sec - 1 - sec)
        right_on = jnp.logical_and(inner, jnp.logical_and(right_g >= 0, right_g < kvl))
        left_on = jnp.logical_and(inner, jnp.logical_and(left_g >= 0, left_g < kvl))
        rg, lg = jnp.clip(right_g, 0, kvl - 1), jnp.clip(left_g, 0, kvl - 1)

        def step(t, carry):
            right = n_sec - 1 - t

            @pl.when(jnp.logical_and(right > sec, right_on))
            def _():
                right_copy(right, rg).wait_recv()
                part[right, rg] = (
                    part[right, rg].astype(F32) + rec_r[right, rg].astype(F32)
                ).astype(BF16)
                right_copy(right, rg).start()

            @pl.when(jnp.logical_and(t < sec, left_on))
            def _():
                left_copy(t, lg).wait_recv()
                part[t, lg] = (part[t, lg].astype(F32) + rec_l[t, lg].astype(F32)).astype(BF16)
                left_copy(t, lg).start()

            return carry

        lax.fori_loop(0, n_sec, step, 0)

    def finish(g):
        @pl.when(sec > 0)
        def _():
            right_copy(sec, g).wait_recv()
            own[g] += rec_r[sec, g].astype(F32)

        @pl.when(sec < n_sec - 1)
        def _():
            left_copy(sec, g).wait_recv()
            own[g] += rec_l[sec, g].astype(F32)

        key_out[:, g * HD : (g + 1) * HD] = own[g, 0]
        value_out[:, g * HD : (g + 1) * HD] = own[g, 1]

    unpack(0)
    pass_one(0)
    for g in range(1, kvl):
        unpack(g)
    pass_two(0)
    if kvl > 1:
        pass_one(1)
    for g in range(1, kvl):
        if g + 1 < kvl:
            pass_one(g + 1)
        pass_two(g)
        relay(g)

    width = group * HD
    for g in range(kvl):
        for d in range(1, n_key):
            dq_copy(d, g).wait_recv()
        total = dqb[g, key].astype(F32)
        for d in range(1, n_key):
            total = total + dqr[d - 1, g].astype(F32)
        qlow[:, g * width : (g + 1) * width] = total.astype(BF16)
    w_load.wait()
    wide = w_v.shape[0]
    tile = 512

    def columns(i, carry):
        first = pl.multiple_of(i * tile, tile)
        product = dot(qlow[...], w_v[pl.ds(first, tile), :], NT).astype(BF16)
        for hh in range(n_head):
            pin[hh, :, pl.ds(first, tile)] = product[hh * block_out : (hh + 1) * block_out]
        return carry

    half = wide // tile // 2
    lax.fori_loop(0, half, columns, 0)
    relay(kvl)
    lax.fori_loop(half, wide // tile, columns, 0)
    for d in range(1, n_head):
        in_copy(d).start()
    for stage in range(kvl + 1, kvl + n_sec - 2):
        relay(stage)
    for g in range(kvl):
        finish(g)

    for d in range(1, n_head):
        in_copy(d).wait_recv()
    total = pin[head].astype(F32)
    for d in range(1, n_head):
        total = total + pin_r[d - 1].astype(F32)
    in_out[...] = total.astype(BF16)

    for g in range(kvl):
        for d in range(1, n_key):
            st_copy(d, g).wait_send()
            dq_copy(d, g).wait_send()

        def drain(c, carry, g=g):
            @pl.when(c > sec)
            def _():
                right_copy(c, g).wait_send()

            @pl.when(c < sec)
            def _():
                left_copy(c, g).wait_send()

            return carry

        lax.fori_loop(0, n_sec, drain, 0)
    for d in range(1, n_head):
        in_copy(d).wait_send()


def hand_out(*refs):
    ins, outs, held, sem = refs[:3], refs[3:6], refs[6:9], refs[9]
    come = [pltpu.make_async_copy(ins[i], held[i], sem.at[0, i]) for i in range(3)]
    leave = [pltpu.make_async_copy(held[i], outs[i], sem.at[1, i]) for i in range(3)]
    for copy in come:
        copy.start()
    for i in range(3):
        come[i].wait()
        leave[i].start()
    for copy in leave:
        copy.wait()


def body(n_sec, n_head, n_key, queries, attn_grad, query_weight, kc, ke, vc, ve):
    rows, cols = queries.shape[1:]
    wide = query_weight.shape[1]
    positions, kv_cols = kc.shape
    kvl = kv_cols // HD
    group_rows = cols // kv_cols * rows
    rows_c = positions // n_sec
    block_out = rows // (n_head * n_key)
    group_cols = cols // kvl
    vmem = pltpu.VMEM
    dma = pltpu.SemaphoreType.DMA
    anywhere = pl.BlockSpec(memory_space=pl.ANY)
    in_vmem = pl.BlockSpec(memory_space=pltpu.VMEM)
    results = pl.pallas_call(
        functools.partial(kernel, n_sec, n_head, n_key),
        out_shape=(
            jax.ShapeDtypeStruct((block_out, wide), BF16),
            jax.ShapeDtypeStruct((rows_c, kv_cols), F32),
            jax.ShapeDtypeStruct((rows_c, kv_cols), F32),
        ),
        in_specs=[anywhere] * 7,
        out_specs=(in_vmem, in_vmem, in_vmem),
        scratch_shapes=[
            vmem(ke.T.shape, jnp.int32),
            vmem(ve.T.shape, jnp.int32),
            vmem((wide, cols), BF16),
            vmem((positions, kv_cols), jnp.int32),
            vmem((positions, kv_cols), jnp.int32),
            vmem((kvl, n_sec, rows_c, HD), BF16),
            vmem((kvl, n_sec, rows_c, HD), BF16),
            vmem((kvl, group_rows, HD), BF16),
            vmem((kvl, group_rows, HD), BF16),
            vmem((2, n_sec, rows_c, group_rows), F32),
            vmem((2, n_sec, rows_c, group_rows), F32),
            vmem((2, n_sec, 8, group_rows), F32),
            vmem((n_key, kvl, 8, group_rows), F32),
            vmem((HD, group_rows), F32),
            vmem((kvl, n_key, n_head * block_out, group_cols), BF16),
            vmem((n_key - 1, kvl, n_head * block_out, group_cols), BF16),
            vmem((n_head * block_out, cols), BF16),
            vmem((n_head, block_out, wide), BF16),
            vmem((n_head - 1, block_out, wide), BF16),
            vmem((n_sec, kvl, 2, rows_c, HD), BF16),
            vmem((n_sec, kvl, 2, rows_c, HD), BF16),
            vmem((n_sec, kvl, 2, rows_c, HD), BF16),
            vmem((kvl, 2, rows_c, HD), F32),
            dma((2,)),
            dma((2, kvl)),
            dma((2, kvl, cols // kv_cols)),
            dma,
            dma((n_key, kvl)),
            dma((n_key, kvl)),
            dma((n_key, kvl)),
            dma((n_key, kvl)),
            dma((n_head,)),
            dma((n_head,)),
            dma((n_sec, kvl)),
            dma((n_sec, kvl)),
            dma((n_sec, kvl)),
        ],
        compiler_params=pltpu.CompilerParams(
            collective_id=0, has_side_effects=True, vmem_limit_bytes=58 * 1024 * 1024
        ),
    )(queries[0], attn_grad[0], query_weight[0], kc, ke.T, vc, ve.T)
    input_grad, key_grad, value_grad = pl.pallas_call(
        hand_out,
        out_shape=tuple(jax.ShapeDtypeStruct(r.shape, r.dtype) for r in results),
        in_specs=[anywhere] * 3,
        out_specs=(anywhere,) * 3,
        scratch_shapes=[vmem(r.shape, r.dtype) for r in results] + [dma((2, 3))],
        compiler_params=pltpu.CompilerParams(vmem_limit_bytes=62 * 1024 * 1024),
    )(*results)
    return input_grad[None], key_grad, value_grad


def solution(mesh):
    shape = mesh.shape
    return jax.shard_map(
        functools.partial(body, shape["section"], shape["head"], shape["key"]),
        mesh=mesh,
        in_specs=(
            P("section", None, "head"),
            P("section", None, "head"),
            P("section", None, "head"),
            P("key", "head"),
            P("key", "head"),
            P("key", "head"),
            P("key", "head"),
        ),
        out_specs=(
            P("section", ("head", "key"), None),
            P(("key", "section"), "head"),
            P(("key", "section"), "head"),
        ),
        check_vma=False,
    )
```

```python
import functools

import jax
import jax.numpy as jnp
from jax import lax
from jax.experimental import pallas as pl
from jax.experimental.pallas import tpu as pltpu
from jax.sharding import PartitionSpec as P

HD = 128
LOG2E = 1.4426950408889634
MESH = pl.DeviceIdType.MESH
F32 = jnp.float32
BF16 = jnp.bfloat16
NT = (((1,), (1,)), ((), ()))
NN = (((1,), (0,)), ((), ()))
TN = (((0,), (0,)), ((), ()))


def dot(a, b, dims):
    return lax.dot_general(a, b, dims, preferred_element_type=F32)


def kernel(
    n_sec, n_head, n_key,
    q_hbm, do_hbm, w_hbm, kc_hbm, ke_hbm, vc_hbm, ve_hbm,
    in_out, key_out, value_out,
    ke, ve, w_v, kc, vc, kd, vd, qs, dos, e_buf, gp_buf,
    blk, st, dq_t, dqb, dqr, qlow, pin, pin_r,
    part, rec_r, rec_l, own,
    exp_sem, code_sem, row_sem, w_sem, st_ss, st_rs, dq_ss, dq_rs, in_ss, in_rs, sec_ss, r_rs, l_rs,
):
    sec = lax.axis_index("section")
    head = lax.axis_index("head")
    key = lax.axis_index("key")
    kvl, _, rows_c, _ = kd.shape
    group_rows = qs.shape[1]
    rows = q_hbm.shape[0]
    group = group_rows // rows
    blk_rows = kc.shape[0] // ke.shape[1]
    block_out = in_out.shape[0]
    scale = HD ** -0.5
    c0 = scale * LOG2E

    barrier = pltpu.get_barrier_semaphore()
    for d in range(1, n_key):
        pl.semaphore_signal(
            barrier, inc=1, device_id={"key": lax.rem(key + d, n_key)}, device_id_type=MESH
        )
    for d in range(1, n_head):
        pl.semaphore_signal(
            barrier, inc=1, device_id={"head": lax.rem(head + d, n_head)}, device_id_type=MESH
        )

    @pl.when(sec > 0)
    def _():
        pl.semaphore_signal(barrier, inc=1, device_id={"section": sec - 1}, device_id_type=MESH)

    @pl.when(sec < n_sec - 1)
    def _():
        pl.semaphore_signal(barrier, inc=1, device_id={"section": sec + 1}, device_id_type=MESH)

    def code_load(i, g):
        src, dst = ((kc_hbm, kc), (vc_hbm, vc))[i]
        cols = pl.ds(g * HD, HD)
        return pltpu.make_async_copy(src.at[:, cols], dst.at[:, cols], code_sem.at[i, g])

    def row_load(i, g, h):
        src, dst = ((q_hbm, qs), (do_hbm, dos))[i]
        return pltpu.make_async_copy(
            src.at[:, pl.ds((g * group + h) * HD, HD)],
            dst.at[g, pl.ds(h * rows, rows)],
            row_sem.at[i, g, h],
        )

    exp_loads = [
        pltpu.make_async_copy(ke_hbm, ke, exp_sem.at[0]),
        pltpu.make_async_copy(ve_hbm, ve, exp_sem.at[1]),
    ]
    w_load = pltpu.make_async_copy(w_hbm, w_v, w_sem)
    for copy in exp_loads:
        copy.start()
    for g in range(kvl):
        for i in range(2):
            code_load(i, g).start()
            for h in range(group):
                row_load(i, g, h).start()

    def st_copy(d, g):
        return pltpu.make_async_remote_copy(
            src_ref=st.at[0, g], dst_ref=st.at[d, g],
            send_sem=st_ss.at[d, g], recv_sem=st_rs.at[d, g],
            device_id={"key": lax.rem(key + d, n_key)}, device_id_type=MESH,
        )

    def dq_copy(d, g):
        to = lax.rem(key + d, n_key)
        return pltpu.make_async_remote_copy(
            src_ref=dqb.at[g, to], dst_ref=dqr.at[d - 1, g],
            send_sem=dq_ss.at[d, g], recv_sem=dq_rs.at[d, g],
            device_id={"key": to}, device_id_type=MESH,
        )

    def in_copy(d):
        to = lax.rem(head + d, n_head)
        return pltpu.make_async_remote_copy(
            src_ref=pin.at[to], dst_ref=pin_r.at[d - 1],
            send_sem=in_ss.at[d], recv_sem=in_rs.at[d],
            device_id={"head": to}, device_id_type=MESH,
        )

    def right_copy(c, g):
        return pltpu.make_async_remote_copy(
            src_ref=part.at[c, g], dst_ref=rec_r.at[c, g],
            send_sem=sec_ss.at[c, g], recv_sem=r_rs.at[c, g],
            device_id={"section": jnp.minimum(sec + 1, n_sec - 1)}, device_id_type=MESH,
        )

    def left_copy(c, g):
        return pltpu.make_async_remote_copy(
            src_ref=part.at[c, g], dst_ref=rec_l.at[c, g],
            send_sem=sec_ss.at[c, g], recv_sem=l_rs.at[c, g],
            device_id={"section": jnp.maximum(sec - 1, 0)}, device_id_type=MESH,
        )

    def dequantize(codes, exps, out, g):
        factors = lax.shift_left(jnp.int32(1), exps[...] + 16).astype(F32) * (2.0 ** -16)
        for b in range(exps.shape[1]):
            first = b * blk_rows
            block = codes[first : first + blk_rows, g * HD : (g + 1) * HD].astype(F32)
            at = first % rows_c
            out[g, first // rows_c, at : at + blk_rows, :] = (
                block * factors[g : g + 1, b : b + 1]
            ).astype(BF16)

    def unpack(g):
        for i, (codes, exps, out) in enumerate(((kc, ke, kd), (vc, ve, vd))):
            if g == 0:
                exp_loads[i].wait()
            code_load(i, g).wait()
            dequantize(codes, exps, out, g)
            for h in range(group):
                row_load(i, g, h).wait()

    def by_chunks(most, work, after=None):
        several = most if n_sec % most == 0 else 1

        def step(i, carry):
            for u in range(several):
                work(i * several + u)
            if after is not None:
                for u in range(several):
                    after(i * several + u)
            return carry

        if several == n_sec:
            step(0, 0)
        else:
            lax.fori_loop(0, n_sec // several, step, 0)

    def pass_one(g):
        slot = g % 2

        def chunk(c):
            keys, values = kd[g, c], vd[g, c]
            for h in range(group):
                cols = slice(h * rows, (h + 1) * rows)
                s = dot(keys, qs[g, cols], NT)
                gp = dot(values, dos[g, cols], NT)
                top = jnp.max(s, axis=0, keepdims=True)
                e = jnp.exp2((s - top) * c0)
                e_buf[slot, c, :, cols] = e
                gp_buf[slot, c, :, cols] = gp
                blk[slot, c, 0:1, cols] = top
                blk[slot, c, 1:2, cols] = jnp.sum(e, axis=0, keepdims=True)
                blk[slot, c, 2:3, cols] = jnp.sum(e * gp, axis=0, keepdims=True)

        by_chunks(4, chunk)
        tops = blk[slot, :, 0:1, :]
        top = jnp.max(tops, axis=0)
        weight = jnp.exp2((tops - top[None]) * c0)
        st[0, g, 0:1, :] = top
        st[0, g, 1:2, :] = jnp.sum(blk[slot, :, 1:2, :] * weight, axis=0)
        st[0, g, 2:3, :] = jnp.sum(blk[slot, :, 2:3, :] * weight, axis=0)
        st[0, g, 3:8, :] = jnp.zeros((5, group_rows), F32)
        if g == 0:
            beside = jnp.where(sec > 0, 1, 0) + jnp.where(sec < n_sec - 1, 1, 0)
            pl.semaphore_wait(barrier, n_key - 1 + n_head - 1 + beside)
            w_load.start()

        for d in range(1, n_key):
            st_copy(d, g).start()

    def pass_two(g):
        slot = g % 2
        for d in range(1, n_key):
            st_copy(d, g).wait_recv()
        tops = [st[d, g, 0:1, :] for d in range(n_key)]
        top = functools.reduce(jnp.maximum, tops)
        weights = [jnp.exp2((t - top) * c0) for t in tops]
        total = sum(st[d, g, 1:2, :] * weights[d] for d in range(n_key))
        inverse = 1.0 / total
        delta = sum(st[d, g, 2:3, :] * weights[d] for d in range(n_key)) * inverse
        dq_t[...] = jnp.zeros_like(dq_t)

        def place(t):
            return jnp.where(sec < n_sec // 2, n_sec - 1 - t, t)

        def chunk(t):
            c = place(t)
            alpha = jnp.exp2((blk[slot, c, 0:1, :] - top) * c0) * inverse
            p = e_buf[slot, c] * alpha
            ds = (p * (gp_buf[slot, c] - delta)).astype(BF16)
            value_part = dot(p.astype(BF16), dos[g], NN)
            key_part = dot(ds, qs[g], NN) * scale
            dq_t[...] += dot(kd[g, c], ds, TN)
            part[c, g, 0] = key_part.astype(BF16)
            part[c, g, 1] = value_part.astype(BF16)

        def send(t):
            c = place(t)

            @pl.when(jnp.logical_and(sec == 0, c > 0))
            def _():
                right_copy(c, g).start()

            @pl.when(jnp.logical_and(sec == n_sec - 1, c < n_sec - 1))
            def _():
                left_copy(c, g).start()

        by_chunks(2, chunk, send)
        dq = (jnp.transpose(dq_t[...]) * scale).astype(BF16)
        for k in range(n_key):
            for hh in range(n_head):
                for h in range(group):
                    first = h * rows + (hh * n_key + k) * block_out
                    dqb[g, k, hh * block_out : (hh + 1) * block_out, h * HD : (h + 1) * HD] = dq[
                        first : first + block_out
                    ]
        for d in range(1, n_key):
            dq_copy(d, g).start()

    def relay(stage):
        inner = jnp.logical_and(sec > 0, sec < n_sec - 1)
        right_g, left_g = stage - sec, stage - (n_sec - 1 - sec)
        right_on = jnp.logical_and(inner, jnp.logical_and(right_g >= 0, right_g < kvl))
        left_on = jnp.logical_and(inner, jnp.logical_and(left_g >= 0, left_g < kvl))
        rg, lg = jnp.clip(right_g, 0, kvl - 1), jnp.clip(left_g, 0, kvl - 1)

        def step(t, carry):
            right = n_sec - 1 - t

            @pl.when(jnp.logical_and(right > sec, right_on))
            def _():
                right_copy(right, rg).wait_recv()
                part[right, rg] = (
                    part[right, rg].astype(F32) + rec_r[right, rg].astype(F32)
                ).astype(BF16)
                right_copy(right, rg).start()

            @pl.when(jnp.logical_and(t < sec, left_on))
            def _():
                left_copy(t, lg).wait_recv()
                part[t, lg] = (part[t, lg].astype(F32) + rec_l[t, lg].astype(F32)).astype(BF16)
                left_copy(t, lg).start()

            return carry

        lax.fori_loop(0, n_sec, step, 0)

    def finish(g):
        own[...] = part[sec, g].astype(F32)

        @pl.when(sec > 0)
        def _():
            right_copy(sec, g).wait_recv()
            own[...] += rec_r[sec, g].astype(F32)

        @pl.when(sec < n_sec - 1)
        def _():
            left_copy(sec, g).wait_recv()
            own[...] += rec_l[sec, g].astype(F32)

        key_out[:, g * HD : (g + 1) * HD] = own[0]
        value_out[:, g * HD : (g + 1) * HD] = own[1]

    unpack(0)
    pass_one(0)
    for g in range(1, kvl):
        unpack(g)
    pass_two(0)
    if kvl > 1:
        pass_one(1)
    for g in range(1, kvl):
        if g + 1 < kvl:
            pass_one(g + 1)
        pass_two(g)
        relay(g)

    width = group * HD
    for g in range(kvl):
        for d in range(1, n_key):
            dq_copy(d, g).wait_recv()
        total = dqb[g, key].astype(F32)
        for d in range(1, n_key):
            total = total + dqr[d - 1, g].astype(F32)
        qlow[:, g * width : (g + 1) * width] = total.astype(BF16)
    w_load.wait()
    wide = w_v.shape[0]
    tile = 512

    def columns(i, carry):
        first = pl.multiple_of(i * tile, tile)
        product = dot(qlow[...], w_v[pl.ds(first, tile), :], NT).astype(BF16)
        for hh in range(n_head):
            pin[hh, :, pl.ds(first, tile)] = product[hh * block_out : (hh + 1) * block_out]
        return carry

    half = wide // tile // 2
    lax.fori_loop(0, half, columns, 0)
    relay(kvl)
    lax.fori_loop(half, wide // tile, columns, 0)
    for d in range(1, n_head):
        in_copy(d).start()
    for stage in range(kvl + 1, kvl + n_sec - 2):
        relay(stage)
    for g in range(kvl):
        finish(g)

    for d in range(1, n_head):
        in_copy(d).wait_recv()
    total = pin[head].astype(F32)
    for d in range(1, n_head):
        total = total + pin_r[d - 1].astype(F32)
    in_out[...] = total.astype(BF16)

    for g in range(kvl):
        for d in range(1, n_key):
            st_copy(d, g).wait_send()
            dq_copy(d, g).wait_send()

        def drain(c, carry, g=g):
            @pl.when(c > sec)
            def _():
                right_copy(c, g).wait_send()

            @pl.when(c < sec)
            def _():
                left_copy(c, g).wait_send()

            return carry

        lax.fori_loop(0, n_sec, drain, 0)
    for d in range(1, n_head):
        in_copy(d).wait_send()


def hand_out(*refs):
    ins, outs, held, sem = refs[:3], refs[3:6], refs[6:9], refs[9]
    come = [pltpu.make_async_copy(ins[i], held[i], sem.at[0, i]) for i in range(3)]
    leave = [pltpu.make_async_copy(held[i], outs[i], sem.at[1, i]) for i in range(3)]
    for copy in come:
        copy.start()
    for i in range(3):
        come[i].wait()
        leave[i].start()
    for copy in leave:
        copy.wait()


def body(n_sec, n_head, n_key, queries, attn_grad, query_weight, kc, ke, vc, ve):
    rows, cols = queries.shape[1:]
    wide = query_weight.shape[1]
    positions, kv_cols = kc.shape
    kvl = kv_cols // HD
    group_rows = cols // kv_cols * rows
    rows_c = positions // n_sec
    block_out = rows // (n_head * n_key)
    group_cols = cols // kvl
    vmem = pltpu.VMEM
    dma = pltpu.SemaphoreType.DMA
    anywhere = pl.BlockSpec(memory_space=pl.ANY)
    in_vmem = pl.BlockSpec(memory_space=pltpu.VMEM)
    results = pl.pallas_call(
        functools.partial(kernel, n_sec, n_head, n_key),
        out_shape=(
            jax.ShapeDtypeStruct((block_out, wide), BF16),
            jax.ShapeDtypeStruct((rows_c, kv_cols), F32),
            jax.ShapeDtypeStruct((rows_c, kv_cols), F32),
        ),
        in_specs=[anywhere] * 7,
        out_specs=(in_vmem, in_vmem, in_vmem),
        scratch_shapes=[
            vmem(ke.T.shape, jnp.int32),
            vmem(ve.T.shape, jnp.int32),
            vmem((wide, cols), BF16),
            vmem((positions, kv_cols), jnp.int32),
            vmem((positions, kv_cols), jnp.int32),
            vmem((kvl, n_sec, rows_c, HD), BF16),
            vmem((kvl, n_sec, rows_c, HD), BF16),
            vmem((kvl, group_rows, HD), BF16),
            vmem((kvl, group_rows, HD), BF16),
            vmem((2, n_sec, rows_c, group_rows), F32),
            vmem((2, n_sec, rows_c, group_rows), F32),
            vmem((2, n_sec, 8, group_rows), F32),
            vmem((n_key, kvl, 8, group_rows), F32),
            vmem((HD, group_rows), F32),
            vmem((kvl, n_key, n_head * block_out, group_cols), BF16),
            vmem((n_key - 1, kvl, n_head * block_out, group_cols), BF16),
            vmem((n_head * block_out, cols), BF16),
            vmem((n_head, block_out, wide), BF16),
            vmem((n_head - 1, block_out, wide), BF16),
            vmem((n_sec, kvl, 2, rows_c, HD), BF16),
            vmem((n_sec, kvl, 2, rows_c, HD), BF16),
            vmem((n_sec, kvl, 2, rows_c, HD), BF16),
            vmem((2, rows_c, HD), F32),
            dma((2,)),
            dma((2, kvl)),
            dma((2, kvl, cols // kv_cols)),
            dma,
            dma((n_key, kvl)),
            dma((n_key, kvl)),
            dma((n_key, kvl)),
            dma((n_key, kvl)),
            dma((n_head,)),
            dma((n_head,)),
            dma((n_sec, kvl)),
            dma((n_sec, kvl)),
            dma((n_sec, kvl)),
        ],
        compiler_params=pltpu.CompilerParams(
            collective_id=0, has_side_effects=True, vmem_limit_bytes=58 * 1024 * 1024
        ),
    )(queries[0], attn_grad[0], query_weight[0], kc, ke.T, vc, ve.T)
    input_grad, key_grad, value_grad = pl.pallas_call(
        hand_out,
        out_shape=tuple(jax.ShapeDtypeStruct(r.shape, r.dtype) for r in results),
        in_specs=[anywhere] * 3,
        out_specs=(anywhere,) * 3,
        scratch_shapes=[vmem(r.shape, r.dtype) for r in results] + [dma((2, 3))],
        compiler_params=pltpu.CompilerParams(vmem_limit_bytes=62 * 1024 * 1024),
    )(*results)
    return input_grad[None], key_grad, value_grad


def solution(mesh):
    shape = mesh.shape
    return jax.shard_map(
        functools.partial(body, shape["section"], shape["head"], shape["key"]),
        mesh=mesh,
        in_specs=(
            P("section", None, "head"),
            P("section", None, "head"),
            P("section", None, "head"),
            P("key", "head"),
            P("key", "head"),
            P("key", "head"),
            P("key", "head"),
        ),
        out_specs=(
            P("section", ("head", "key"), None),
            P(("key", "section"), "head"),
            P(("key", "section"), "head"),
        ),
        check_vma=False,
    )
```

```python
import functools

import jax
import jax.numpy as jnp
from jax import lax
from jax.experimental import pallas as pl
from jax.experimental.pallas import tpu as pltpu
from jax.sharding import PartitionSpec as P

HD = 128
LOG2E = 1.4426950408889634
MESH = pl.DeviceIdType.MESH
F32 = jnp.float32
BF16 = jnp.bfloat16
NT = (((1,), (1,)), ((), ()))
NN = (((1,), (0,)), ((), ()))
TN = (((0,), (0,)), ((), ()))


def dot(a, b, dims):
    return lax.dot_general(a, b, dims, preferred_element_type=F32)


def kernel(
    n_sec, n_head, n_key,
    q_hbm, do_hbm, w_hbm, kc_hbm, ke_hbm, vc_hbm, ve_hbm,
    in_out, key_out, value_out,
    ke, ve, w_v, kc, vc, kd, vd, qs, dos, e_buf, gp_buf,
    blk, st, dq_t, dqb, dqr, qlow, pin, pin_r,
    part, rec_r, rec_l, own, h_q, h_do, h_st, h_st_out,
    exp_sem, code_sem, row_sem, w_sem, st_ss, st_rs, dq_ss, dq_rs, in_ss, in_rs, sec_ss, r_rs, l_rs, h_ss, h_rs,
):
    sec = lax.axis_index("section")
    head = lax.axis_index("head")
    key = lax.axis_index("key")
    kvl, _, rows_c, _ = kd.shape
    group_rows = qs.shape[1]
    rows = q_hbm.shape[0]
    group = group_rows // rows
    blk_rows = kc.shape[0] // ke.shape[1]
    block_out = in_out.shape[0]
    scale = HD ** -0.5
    c0 = scale * LOG2E
    shared = kvl - 1 if n_sec >= 4 else -1
    ends = jnp.logical_or(sec == 0, sec == n_sec - 1)
    helpers = jnp.logical_or(sec == 1, sec == n_sec - 2)

    barrier = pltpu.get_barrier_semaphore()
    for d in range(1, n_key):
        pl.semaphore_signal(
            barrier, inc=1, device_id={"key": lax.rem(key + d, n_key)}, device_id_type=MESH
        )
    for d in range(1, n_head):
        pl.semaphore_signal(
            barrier, inc=1, device_id={"head": lax.rem(head + d, n_head)}, device_id_type=MESH
        )

    @pl.when(sec > 0)
    def _():
        pl.semaphore_signal(barrier, inc=1, device_id={"section": sec - 1}, device_id_type=MESH)

    @pl.when(sec < n_sec - 1)
    def _():
        pl.semaphore_signal(barrier, inc=1, device_id={"section": sec + 1}, device_id_type=MESH)

    def code_load(i, g):
        src, dst = ((kc_hbm, kc), (vc_hbm, vc))[i]
        cols = pl.ds(g * HD, HD)
        return pltpu.make_async_copy(src.at[:, cols], dst.at[:, cols], code_sem.at[i, g])

    def row_load(i, g, h):
        src, dst = ((q_hbm, qs), (do_hbm, dos))[i]
        return pltpu.make_async_copy(
            src.at[:, pl.ds((g * group + h) * HD, HD)],
            dst.at[g, pl.ds(h * rows, rows)],
            row_sem.at[i, g, h],
        )

    exp_loads = [
        pltpu.make_async_copy(ke_hbm, ke, exp_sem.at[0]),
        pltpu.make_async_copy(ve_hbm, ve, exp_sem.at[1]),
    ]
    w_load = pltpu.make_async_copy(w_hbm, w_v, w_sem)
    for copy in exp_loads:
        copy.start()
    for g in range(kvl):
        for i in range(2):
            code_load(i, g).start()
            for h in range(group):
                if g == 0 or g != shared:
                    row_load(i, g, h).start()
                if g == 0 and shared > 0:
                    row_load(i, shared, h).start()

    def help_copy(i):
        src, dst = ((qs.at[shared], h_q), (dos.at[shared], h_do), (h_st_out, h_st))[i]
        return pltpu.make_async_remote_copy(
            src_ref=src, dst_ref=dst, send_sem=h_ss.at[i], recv_sem=h_rs.at[i],
            device_id={"section": jnp.where(sec == 0, 1, n_sec - 2)}, device_id_type=MESH,
        )

    def st_copy(d, g):
        return pltpu.make_async_remote_copy(
            src_ref=st.at[0, g], dst_ref=st.at[d, g],
            send_sem=st_ss.at[d, g], recv_sem=st_rs.at[d, g],
            device_id={"key": lax.rem(key + d, n_key)}, device_id_type=MESH,
        )

    def dq_copy(d, g):
        to = lax.rem(key + d, n_key)
        return pltpu.make_async_remote_copy(
            src_ref=dqb.at[g, to], dst_ref=dqr.at[d - 1, g],
            send_sem=dq_ss.at[d, g], recv_sem=dq_rs.at[d, g],
            device_id={"key": to}, device_id_type=MESH,
        )

    def in_copy(d):
        to = lax.rem(head + d, n_head)
        return pltpu.make_async_remote_copy(
            src_ref=pin.at[to], dst_ref=pin_r.at[d - 1],
            send_sem=in_ss.at[d], recv_sem=in_rs.at[d],
            device_id={"head": to}, device_id_type=MESH,
        )

    def right_copy(c, g):
        return pltpu.make_async_remote_copy(
            src_ref=part.at[c, g], dst_ref=rec_r.at[c, g],
            send_sem=sec_ss.at[c, g], recv_sem=r_rs.at[c, g],
            device_id={"section": jnp.minimum(sec + 1, n_sec - 1)}, device_id_type=MESH,
        )

    def left_copy(c, g):
        return pltpu.make_async_remote_copy(
            src_ref=part.at[c, g], dst_ref=rec_l.at[c, g],
            send_sem=sec_ss.at[c, g], recv_sem=l_rs.at[c, g],
            device_id={"section": jnp.maximum(sec - 1, 0)}, device_id_type=MESH,
        )

    def dequantize(codes, exps, out, g):
        factors = lax.shift_left(jnp.int32(1), exps[...] + 16).astype(F32) * (2.0 ** -16)
        for b in range(exps.shape[1]):
            first = b * blk_rows
            block = codes[first : first + blk_rows, g * HD : (g + 1) * HD].astype(F32)
            at = first % rows_c
            out[g, first // rows_c, at : at + blk_rows, :] = (
                block * factors[g : g + 1, b : b + 1]
            ).astype(BF16)

    def unpack(g):
        for i, (codes, exps, out) in enumerate(((kc, ke, kd), (vc, ve, vd))):
            if g == 0:
                exp_loads[i].wait()
            code_load(i, g).wait()
            dequantize(codes, exps, out, g)
            for h in range(group):
                if g == 0 or g != shared:
                    row_load(i, g, h).wait()
                if g == 0 and shared > 0:
                    row_load(i, shared, h).wait()

    def by_chunks(most, work, after=None):
        several = most if n_sec % most == 0 else 1

        def step(i, carry):
            for u in range(several):
                work(i * several + u)
            if after is not None:
                for u in range(several):
                    after(i * several + u)
            return carry

        if several == n_sec:
            step(0, 0)
        else:
            lax.fori_loop(0, n_sec // several, step, 0)

    def pass_one(g):
        slot = g % 2

        def chunk(c):
            keys, values = kd[g, c], vd[g, c]
            for h in range(group):
                cols = slice(h * rows, (h + 1) * rows)
                s = dot(keys, qs[g, cols], NT)
                gp = dot(values, dos[g, cols], NT)
                top = jnp.max(s, axis=0, keepdims=True)
                e = jnp.exp2((s - top) * c0)
                e_buf[slot, c, :, cols] = e
                gp_buf[slot, c, :, cols] = gp
                blk[slot, c, 0:1, cols] = top
                blk[slot, c, 1:2, cols] = jnp.sum(e, axis=0, keepdims=True)
                blk[slot, c, 2:3, cols] = jnp.sum(e * gp, axis=0, keepdims=True)

        by_chunks(4, chunk)
        tops = blk[slot, :, 0:1, :]
        top = jnp.max(tops, axis=0)
        weight = jnp.exp2((tops - top[None]) * c0)
        st[0, g, 0:1, :] = top
        st[0, g, 1:2, :] = jnp.sum(blk[slot, :, 1:2, :] * weight, axis=0)
        st[0, g, 2:3, :] = jnp.sum(blk[slot, :, 2:3, :] * weight, axis=0)
        st[0, g, 3:8, :] = jnp.zeros((5, group_rows), F32)
        for d in range(1, n_key):
            st_copy(d, g).start()

    def pass_two(g):
        slot = g % 2
        for d in range(1, n_key):
            st_copy(d, g).wait_recv()
        tops = [st[d, g, 0:1, :] for d in range(n_key)]
        top = functools.reduce(jnp.maximum, tops)
        weights = [jnp.exp2((t - top) * c0) for t in tops]
        total = sum(st[d, g, 1:2, :] * weights[d] for d in range(n_key))
        inverse = 1.0 / total
        delta = sum(st[d, g, 2:3, :] * weights[d] for d in range(n_key)) * inverse
        if g == shared:

            @pl.when(ends)
            def _():
                h_st_out[0:1] = top
                h_st_out[1:2] = inverse
                h_st_out[2:3] = delta
                h_st_out[3:8] = jnp.zeros((5, group_rows), F32)
                help_copy(2).start()

        dq_t[...] = jnp.zeros_like(dq_t)

        def place(t):
            return jnp.where(sec < n_sec // 2, n_sec - 1 - t, t)

        def chunk(t):
            c = place(t)
            alpha = jnp.exp2((blk[slot, c, 0:1, :] - top) * c0) * inverse
            p = e_buf[slot, c] * alpha
            ds = (p * (gp_buf[slot, c] - delta)).astype(BF16)
            value_part = dot(p.astype(BF16), dos[g], NN)
            key_part = dot(ds, qs[g], NN) * scale
            dq_t[...] += dot(kd[g, c], ds, TN)
            part[c, g, 0] = key_part.astype(BF16)
            part[c, g, 1] = value_part.astype(BF16)

        def send(t):
            c = place(t)

            @pl.when(jnp.logical_and(sec == 0, c > 0))
            def _():
                right_copy(c, g).start()

            @pl.when(jnp.logical_and(sec == n_sec - 1, c < n_sec - 1))
            def _():
                left_copy(c, g).start()

        by_chunks(2, chunk, None if g == shared else send)
        dq = (jnp.transpose(dq_t[...]) * scale).astype(BF16)
        for k in range(n_key):
            for hh in range(n_head):
                for h in range(group):
                    first = h * rows + (hh * n_key + k) * block_out
                    dqb[g, k, hh * block_out : (hh + 1) * block_out, h * HD : (h + 1) * HD] = dq[
                        first : first + block_out
                    ]
        for d in range(1, n_key):
            dq_copy(d, g).start()

    def relay(stage):
        inner = jnp.logical_and(sec > 0, sec < n_sec - 1)
        right_g, left_g = stage - sec, stage - (n_sec - 1 - sec)
        right_on = jnp.logical_and(inner, jnp.logical_and(right_g >= 0, right_g < kvl))
        left_on = jnp.logical_and(inner, jnp.logical_and(left_g >= 0, left_g < kvl))
        rg, lg = jnp.clip(right_g, 0, kvl - 1), jnp.clip(left_g, 0, kvl - 1)

        def step(t, carry):
            right = n_sec - 1 - t

            @pl.when(jnp.logical_and(right > sec, right_on))
            def _():
                @pl.when(jnp.logical_not(jnp.logical_and(sec == 1, rg == shared)))
                def _():
                    right_copy(right, rg).wait_recv()
                    part[right, rg] = (
                        part[right, rg].astype(F32) + rec_r[right, rg].astype(F32)
                    ).astype(BF16)

                right_copy(right, rg).start()

            @pl.when(jnp.logical_and(t < sec, left_on))
            def _():
                @pl.when(jnp.logical_not(jnp.logical_and(sec == n_sec - 2, lg == shared)))
                def _():
                    left_copy(t, lg).wait_recv()
                    part[t, lg] = (part[t, lg].astype(F32) + rec_l[t, lg].astype(F32)).astype(BF16)

                left_copy(t, lg).start()

            return carry

        lax.fori_loop(0, n_sec, step, 0)

    def assist():
        for i in range(3):
            help_copy(i).wait_recv()
        top, inverse, delta = h_st[0:1], h_st[1:2], h_st[2:3]

        def step(c, carry):
            @pl.when(jnp.where(sec == 1, c > 0, c < n_sec - 1))
            def _():
                key_part = part[c, shared, 0].astype(F32)
                value_part = part[c, shared, 1].astype(F32)
                for h in range(group):
                    cols = slice(h * rows, (h + 1) * rows)
                    s = dot(kd[shared, c], h_q[cols], NT)
                    gp = dot(vd[shared, c], h_do[cols], NT)
                    p = jnp.exp2((s - top[:, cols]) * c0) * inverse[:, cols]
                    ds = (p * (gp - delta[:, cols])).astype(BF16)
                    key_part += dot(ds, h_q[cols], NN) * scale
                    value_part += dot(p.astype(BF16), h_do[cols], NN)
                part[c, shared, 0] = key_part.astype(BF16)
                part[c, shared, 1] = value_part.astype(BF16)

            return carry

        lax.fori_loop(0, n_sec, step, 0)

    def finish(g):
        own[...] = part[sec, g].astype(F32)

        from_left, from_right = sec > 0, sec < n_sec - 1
        if g == shared:
            from_left = jnp.logical_and(from_left, sec != 1)
            from_right = jnp.logical_and(from_right, sec != n_sec - 2)

        @pl.when(from_left)
        def _():
            right_copy(sec, g).wait_recv()
            own[...] += rec_r[sec, g].astype(F32)

        @pl.when(from_right)
        def _():
            left_copy(sec, g).wait_recv()
            own[...] += rec_l[sec, g].astype(F32)

        key_out[:, g * HD : (g + 1) * HD] = own[0]
        value_out[:, g * HD : (g + 1) * HD] = own[1]

    unpack(0)
    beside = jnp.where(sec > 0, 1, 0) + jnp.where(sec < n_sec - 1, 1, 0)
    pl.semaphore_wait(barrier, n_key - 1 + n_head - 1 + beside)
    if shared >= 0:

        @pl.when(ends)
        def _():
            help_copy(0).start()
            help_copy(1).start()

    w_load.start()
    pass_one(0)
    for g in range(1, kvl):
        unpack(g)
    pass_two(0)
    if kvl > 1:
        pass_one(1)
    for g in range(1, kvl):
        if g + 1 < kvl:
            pass_one(g + 1)
        pass_two(g)
        relay(g)
    if shared >= 0:
        pl.when(helpers)(assist)

    width = group * HD
    for g in range(kvl):
        for d in range(1, n_key):
            dq_copy(d, g).wait_recv()
        total = dqb[g, key].astype(F32)
        for d in range(1, n_key):
            total = total + dqr[d - 1, g].astype(F32)
        qlow[:, g * width : (g + 1) * width] = total.astype(BF16)
    w_load.wait()
    wide = w_v.shape[0]
    tile = 512

    def columns(i, carry):
        first = pl.multiple_of(i * tile, tile)
        product = dot(qlow[...], w_v[pl.ds(first, tile), :], NT).astype(BF16)
        for hh in range(n_head):
            pin[hh, :, pl.ds(first, tile)] = product[hh * block_out : (hh + 1) * block_out]
        return carry

    half = wide // tile // 2
    lax.fori_loop(0, half, columns, 0)
    relay(kvl)
    lax.fori_loop(half, wide // tile, columns, 0)
    for d in range(1, n_head):
        in_copy(d).start()
    for stage in range(kvl + 1, kvl + n_sec - 2):
        relay(stage)
    for g in range(kvl):
        finish(g)

    for d in range(1, n_head):
        in_copy(d).wait_recv()
    total = pin[head].astype(F32)
    for d in range(1, n_head):
        total = total + pin_r[d - 1].astype(F32)
    in_out[...] = total.astype(BF16)

    for g in range(kvl):
        for d in range(1, n_key):
            st_copy(d, g).wait_send()
            dq_copy(d, g).wait_send()

        def drain(c, carry, g=g):
            to_right, to_left = c > sec, c < sec
            if g == shared:
                to_right = jnp.logical_and(to_right, sec != 0)
                to_left = jnp.logical_and(to_left, sec != n_sec - 1)

            @pl.when(to_right)
            def _():
                right_copy(c, g).wait_send()

            @pl.when(to_left)
            def _():
                left_copy(c, g).wait_send()

            return carry

        lax.fori_loop(0, n_sec, drain, 0)
    for d in range(1, n_head):
        in_copy(d).wait_send()
    if shared >= 0:

        @pl.when(ends)
        def _():
            for i in range(3):
                help_copy(i).wait_send()


def hand_out(*refs):
    ins, outs, held, sem = refs[:3], refs[3:6], refs[6:9], refs[9]
    come = [pltpu.make_async_copy(ins[i], held[i], sem.at[0, i]) for i in range(3)]
    leave = [pltpu.make_async_copy(held[i], outs[i], sem.at[1, i]) for i in range(3)]
    for copy in come:
        copy.start()
    for i in range(3):
        come[i].wait()
        leave[i].start()
    for copy in leave:
        copy.wait()


def body(n_sec, n_head, n_key, queries, attn_grad, query_weight, kc, ke, vc, ve):
    rows, cols = queries.shape[1:]
    wide = query_weight.shape[1]
    positions, kv_cols = kc.shape
    kvl = kv_cols // HD
    group_rows = cols // kv_cols * rows
    rows_c = positions // n_sec
    block_out = rows // (n_head * n_key)
    group_cols = cols // kvl
    vmem = pltpu.VMEM
    dma = pltpu.SemaphoreType.DMA
    anywhere = pl.BlockSpec(memory_space=pl.ANY)
    in_vmem = pl.BlockSpec(memory_space=pltpu.VMEM)
    results = pl.pallas_call(
        functools.partial(kernel, n_sec, n_head, n_key),
        out_shape=(
            jax.ShapeDtypeStruct((block_out, wide), BF16),
            jax.ShapeDtypeStruct((rows_c, kv_cols), F32),
            jax.ShapeDtypeStruct((rows_c, kv_cols), F32),
        ),
        in_specs=[anywhere] * 7,
        out_specs=(in_vmem, in_vmem, in_vmem),
        scratch_shapes=[
            vmem(ke.T.shape, jnp.int32),
            vmem(ve.T.shape, jnp.int32),
            vmem((wide, cols), BF16),
            vmem((positions, kv_cols), jnp.int32),
            vmem((positions, kv_cols), jnp.int32),
            vmem((kvl, n_sec, rows_c, HD), BF16),
            vmem((kvl, n_sec, rows_c, HD), BF16),
            vmem((kvl, group_rows, HD), BF16),
            vmem((kvl, group_rows, HD), BF16),
            vmem((2, n_sec, rows_c, group_rows), F32),
            vmem((2, n_sec, rows_c, group_rows), F32),
            vmem((2, n_sec, 8, group_rows), F32),
            vmem((n_key, kvl, 8, group_rows), F32),
            vmem((HD, group_rows), F32),
            vmem((kvl, n_key, n_head * block_out, group_cols), BF16),
            vmem((n_key - 1, kvl, n_head * block_out, group_cols), BF16),
            vmem((n_head * block_out, cols), BF16),
            vmem((n_head, block_out, wide), BF16),
            vmem((n_head - 1, block_out, wide), BF16),
            vmem((n_sec, kvl, 2, rows_c, HD), BF16),
            vmem((n_sec, kvl, 2, rows_c, HD), BF16),
            vmem((n_sec, kvl, 2, rows_c, HD), BF16),
            vmem((2, rows_c, HD), F32),
            vmem((group_rows, HD), BF16),
            vmem((group_rows, HD), BF16),
            vmem((8, group_rows), F32),
            vmem((8, group_rows), F32),
            dma((2,)),
            dma((2, kvl)),
            dma((2, kvl, cols // kv_cols)),
            dma,
            dma((n_key, kvl)),
            dma((n_key, kvl)),
            dma((n_key, kvl)),
            dma((n_key, kvl)),
            dma((n_head,)),
            dma((n_head,)),
            dma((n_sec, kvl)),
            dma((n_sec, kvl)),
            dma((n_sec, kvl)),
            dma((3,)),
            dma((3,)),
        ],
        compiler_params=pltpu.CompilerParams(
            collective_id=0, has_side_effects=True, vmem_limit_bytes=58 * 1024 * 1024
        ),
    )(queries[0], attn_grad[0], query_weight[0], kc, ke.T, vc, ve.T)
    input_grad, key_grad, value_grad = pl.pallas_call(
        hand_out,
        out_shape=tuple(jax.ShapeDtypeStruct(r.shape, r.dtype) for r in results),
        in_specs=[anywhere] * 3,
        out_specs=(anywhere,) * 3,
        scratch_shapes=[vmem(r.shape, r.dtype) for r in results] + [dma((2, 3))],
        compiler_params=pltpu.CompilerParams(vmem_limit_bytes=62 * 1024 * 1024),
    )(*results)
    return input_grad[None], key_grad, value_grad


def solution(mesh):
    shape = mesh.shape
    return jax.shard_map(
        functools.partial(body, shape["section"], shape["head"], shape["key"]),
        mesh=mesh,
        in_specs=(
            P("section", None, "head"),
            P("section", None, "head"),
            P("section", None, "head"),
            P("key", "head"),
            P("key", "head"),
            P("key", "head"),
            P("key", "head"),
        ),
        out_specs=(
            P("section", ("head", "key"), None),
            P(("key", "section"), "head"),
            P(("key", "section"), "head"),
        ),
        check_vma=False,
    )
```

```python
import functools

import jax
import jax.numpy as jnp
from jax import lax
from jax.experimental import pallas as pl
from jax.experimental.pallas import tpu as pltpu
from jax.sharding import PartitionSpec as P

HD = 128
LOG2E = 1.4426950408889634
MESH = pl.DeviceIdType.MESH
F32 = jnp.float32
BF16 = jnp.bfloat16
NT = (((1,), (1,)), ((), ()))
NN = (((1,), (0,)), ((), ()))
TN = (((0,), (0,)), ((), ()))


def dot(a, b, dims):
    return lax.dot_general(a, b, dims, preferred_element_type=F32)


def kernel(
    n_sec, n_head, n_key,
    q_hbm, do_hbm, w_hbm, kc_hbm, ke_hbm, vc_hbm, ve_hbm,
    in_out, key_out, value_out,
    ke, ve, w_v, kc, vc, kd, vd, qs, dos, e_buf, gp_buf,
    blk, st, dq_t, dqb, dqr, qlow, pin, pin_r,
    part, rec_r, rec_l, own, h_q, h_do, h_st, h_st_out,
    exp_sem, code_sem, row_sem, w_sem, st_ss, st_rs, dq_ss, dq_rs, in_ss, in_rs, sec_ss, r_rs, l_rs, h_ss, h_rs,
):
    sec = lax.axis_index("section")
    head = lax.axis_index("head")
    key = lax.axis_index("key")
    kvl, _, rows_c, _ = kd.shape
    group_rows = qs.shape[1]
    rows = q_hbm.shape[0]
    group = group_rows // rows
    blk_rows = kc.shape[0] // ke.shape[1]
    block_out = in_out.shape[0]
    scale = HD ** -0.5
    c0 = scale * LOG2E
    shared = kvl - 1 if n_sec >= 4 else -1
    ends = jnp.logical_or(sec == 0, sec == n_sec - 1)
    helpers = jnp.logical_or(sec == 1, sec == n_sec - 2)

    barrier = pltpu.get_barrier_semaphore()
    for d in range(1, n_key):
        pl.semaphore_signal(
            barrier, inc=1, device_id={"key": lax.rem(key + d, n_key)}, device_id_type=MESH
        )
    for d in range(1, n_head):
        pl.semaphore_signal(
            barrier, inc=1, device_id={"head": lax.rem(head + d, n_head)}, device_id_type=MESH
        )

    @pl.when(sec > 0)
    def _():
        pl.semaphore_signal(barrier, inc=1, device_id={"section": sec - 1}, device_id_type=MESH)

    @pl.when(sec < n_sec - 1)
    def _():
        pl.semaphore_signal(barrier, inc=1, device_id={"section": sec + 1}, device_id_type=MESH)

    def code_load(i, g):
        src, dst = ((kc_hbm, kc), (vc_hbm, vc))[i]
        cols = pl.ds(g * HD, HD)
        return pltpu.make_async_copy(src.at[:, cols], dst.at[:, cols], code_sem.at[i, g])

    def row_load(i, g, h):
        src, dst = ((q_hbm, qs), (do_hbm, dos))[i]
        return pltpu.make_async_copy(
            src.at[:, pl.ds((g * group + h) * HD, HD)],
            dst.at[g, pl.ds(h * rows, rows)],
            row_sem.at[i, g, h],
        )

    exp_loads = [
        pltpu.make_async_copy(ke_hbm, ke, exp_sem.at[0]),
        pltpu.make_async_copy(ve_hbm, ve, exp_sem.at[1]),
    ]
    w_load = pltpu.make_async_copy(w_hbm, w_v, w_sem)
    for copy in exp_loads:
        copy.start()
    for g in range(kvl):
        for i in range(2):
            code_load(i, g).start()
            for h in range(group):
                if g == 0 or g != shared:
                    row_load(i, g, h).start()
                if g == 0 and shared > 0:
                    row_load(i, shared, h).start()

    def help_copy(i):
        src, dst = ((qs.at[shared], h_q), (dos.at[shared], h_do), (h_st_out, h_st))[i]
        return pltpu.make_async_remote_copy(
            src_ref=src, dst_ref=dst, send_sem=h_ss.at[i], recv_sem=h_rs.at[i],
            device_id={"section": jnp.where(sec == 0, 1, n_sec - 2)}, device_id_type=MESH,
        )

    def st_copy(d, g):
        return pltpu.make_async_remote_copy(
            src_ref=st.at[0, g], dst_ref=st.at[d, g],
            send_sem=st_ss.at[d, g], recv_sem=st_rs.at[d, g],
            device_id={"key": lax.rem(key + d, n_key)}, device_id_type=MESH,
        )

    def dq_copy(d, g):
        to = lax.rem(key + d, n_key)
        return pltpu.make_async_remote_copy(
            src_ref=dqb.at[g, to], dst_ref=dqr.at[d - 1, g],
            send_sem=dq_ss.at[d, g], recv_sem=dq_rs.at[d, g],
            device_id={"key": to}, device_id_type=MESH,
        )

    def in_copy(d):
        to = lax.rem(head + d, n_head)
        return pltpu.make_async_remote_copy(
            src_ref=pin.at[to], dst_ref=pin_r.at[d - 1],
            send_sem=in_ss.at[d], recv_sem=in_rs.at[d],
            device_id={"head": to}, device_id_type=MESH,
        )

    def right_copy(c, g):
        return pltpu.make_async_remote_copy(
            src_ref=part.at[c, g], dst_ref=rec_r.at[c, g],
            send_sem=sec_ss.at[c, g], recv_sem=r_rs.at[c, g],
            device_id={"section": jnp.minimum(sec + 1, n_sec - 1)}, device_id_type=MESH,
        )

    def left_copy(c, g):
        return pltpu.make_async_remote_copy(
            src_ref=part.at[c, g], dst_ref=rec_l.at[c, g],
            send_sem=sec_ss.at[c, g], recv_sem=l_rs.at[c, g],
            device_id={"section": jnp.maximum(sec - 1, 0)}, device_id_type=MESH,
        )

    def dequantize(codes, exps, out, g):
        factors = lax.shift_left(jnp.int32(1), exps[...] + 16).astype(F32) * (2.0 ** -16)
        for b in range(exps.shape[1]):
            first = b * blk_rows
            block = codes[first : first + blk_rows, g * HD : (g + 1) * HD].astype(F32)
            at = first % rows_c
            out[g, first // rows_c, at : at + blk_rows, :] = (
                block * factors[g : g + 1, b : b + 1]
            ).astype(BF16)

    def unpack(g):
        for i, (codes, exps, out) in enumerate(((kc, ke, kd), (vc, ve, vd))):
            if g == 0:
                exp_loads[i].wait()
            code_load(i, g).wait()
            dequantize(codes, exps, out, g)
            for h in range(group):
                if g == 0 or g != shared:
                    row_load(i, g, h).wait()
                if g == 0 and shared > 0:
                    row_load(i, shared, h).wait()

    def by_chunks(most, work, after=None):
        several = most if n_sec % most == 0 else 1

        def step(i, carry):
            for u in range(several):
                work(i * several + u)
            if after is not None:
                for u in range(several):
                    after(i * several + u)
            return carry

        if several == n_sec:
            step(0, 0)
        else:
            lax.fori_loop(0, n_sec // several, step, 0)

    def pass_one(g):
        slot = g % 2

        def chunk(c):
            keys, values = kd[g, c], vd[g, c]
            for h in range(group):
                cols = slice(h * rows, (h + 1) * rows)
                s = dot(keys, qs[g, cols], NT)
                gp = dot(values, dos[g, cols], NT)
                top = jnp.max(s, axis=0, keepdims=True)
                e = jnp.exp2((s - top) * c0)
                e_buf[slot, c, :, cols] = e
                gp_buf[slot, c, :, cols] = gp
                blk[slot, c, 0:1, cols] = top
                blk[slot, c, 1:2, cols] = jnp.sum(e, axis=0, keepdims=True)
                blk[slot, c, 2:3, cols] = jnp.sum(e * gp, axis=0, keepdims=True)

        by_chunks(4, chunk)
        tops = blk[slot, :, 0:1, :]
        top = jnp.max(tops, axis=0)
        weight = jnp.exp2((tops - top[None]) * c0)
        st[0, g, 0:1, :] = top
        st[0, g, 1:2, :] = jnp.sum(blk[slot, :, 1:2, :] * weight, axis=0)
        st[0, g, 2:3, :] = jnp.sum(blk[slot, :, 2:3, :] * weight, axis=0)
        st[0, g, 3:8, :] = jnp.zeros((5, group_rows), F32)
        for d in range(1, n_key):
            st_copy(d, g).start()

    def pass_two(g):
        slot = g % 2
        for d in range(1, n_key):
            st_copy(d, g).wait_recv()
        tops = [st[d, g, 0:1, :] for d in range(n_key)]
        top = functools.reduce(jnp.maximum, tops)
        weights = [jnp.exp2((t - top) * c0) for t in tops]
        total = sum(st[d, g, 1:2, :] * weights[d] for d in range(n_key))
        inverse = 1.0 / total
        delta = sum(st[d, g, 2:3, :] * weights[d] for d in range(n_key)) * inverse
        if g == shared:

            @pl.when(ends)
            def _():
                h_st_out[0:1] = top
                h_st_out[1:2] = inverse
                h_st_out[2:3] = delta
                h_st_out[3:8] = jnp.zeros((5, group_rows), F32)
                help_copy(2).start()

        dq_t[...] = jnp.zeros_like(dq_t)

        def place(t):
            return jnp.where(sec < n_sec // 2, n_sec - 1 - t, t)

        def chunk(t):
            c = place(t)
            alpha = jnp.exp2((blk[slot, c, 0:1, :] - top) * c0) * inverse
            p = e_buf[slot, c] * alpha
            ds = (p * (gp_buf[slot, c] - delta)).astype(BF16)
            value_part = dot(p.astype(BF16), dos[g], NN)
            key_part = dot(ds, qs[g], NN) * scale
            dq_t[...] += dot(kd[g, c], ds, TN)
            part[c, g, 0] = key_part.astype(BF16)
            part[c, g, 1] = value_part.astype(BF16)

        def send(t):
            c = place(t)

            @pl.when(jnp.logical_and(sec == 0, c > 0))
            def _():
                right_copy(c, g).start()

            @pl.when(jnp.logical_and(sec == n_sec - 1, c < n_sec - 1))
            def _():
                left_copy(c, g).start()

        by_chunks(2, chunk, None if g == shared else send)
        dq = (jnp.transpose(dq_t[...]) * scale).astype(BF16)
        for k in range(n_key):
            for hh in range(n_head):
                for h in range(group):
                    first = h * rows + (hh * n_key + k) * block_out
                    dqb[g, k, hh * block_out : (hh + 1) * block_out, h * HD : (h + 1) * HD] = dq[
                        first : first + block_out
                    ]
        for d in range(1, n_key):
            dq_copy(d, g).start()

    def relay(stage):
        inner = jnp.logical_and(sec > 0, sec < n_sec - 1)
        right_g, left_g = stage - sec, stage - (n_sec - 1 - sec)
        right_on = jnp.logical_and(inner, jnp.logical_and(right_g >= 0, right_g < kvl))
        left_on = jnp.logical_and(inner, jnp.logical_and(left_g >= 0, left_g < kvl))
        right_on = jnp.logical_and(right_on, jnp.logical_or(sec != 1, right_g != shared))
        left_on = jnp.logical_and(left_on, jnp.logical_or(sec != n_sec - 2, left_g != shared))
        rg, lg = jnp.clip(right_g, 0, kvl - 1), jnp.clip(left_g, 0, kvl - 1)

        def step(t, carry):
            right = n_sec - 1 - t

            @pl.when(jnp.logical_and(right > sec, right_on))
            def _():
                right_copy(right, rg).wait_recv()
                part[right, rg] = (
                    part[right, rg].astype(F32) + rec_r[right, rg].astype(F32)
                ).astype(BF16)
                right_copy(right, rg).start()

            @pl.when(jnp.logical_and(t < sec, left_on))
            def _():
                left_copy(t, lg).wait_recv()
                part[t, lg] = (part[t, lg].astype(F32) + rec_l[t, lg].astype(F32)).astype(BF16)
                left_copy(t, lg).start()

            return carry

        lax.fori_loop(0, n_sec, step, 0)

    def assist():
        for i in range(3):
            help_copy(i).wait_recv()
        top, inverse, delta = h_st[0:1], h_st[1:2], h_st[2:3]

        def step(c, carry):
            @pl.when(jnp.where(sec == 1, c > 0, c < n_sec - 1))
            def _():
                key_part = part[c, shared, 0].astype(F32)
                value_part = part[c, shared, 1].astype(F32)
                for h in range(group):
                    cols = slice(h * rows, (h + 1) * rows)
                    s = dot(kd[shared, c], h_q[cols], NT)
                    gp = dot(vd[shared, c], h_do[cols], NT)
                    p = jnp.exp2((s - top[:, cols]) * c0) * inverse[:, cols]
                    ds = (p * (gp - delta[:, cols])).astype(BF16)
                    key_part += dot(ds, h_q[cols], NN) * scale
                    value_part += dot(p.astype(BF16), h_do[cols], NN)
                part[c, shared, 0] = key_part.astype(BF16)
                part[c, shared, 1] = value_part.astype(BF16)

                @pl.when(jnp.logical_and(sec == 1, c > 1))
                def _():
                    right_copy(c, shared).start()

                @pl.when(jnp.logical_and(sec == n_sec - 2, c < n_sec - 2))
                def _():
                    left_copy(c, shared).start()

            return carry

        lax.fori_loop(0, n_sec, step, 0)

    def finish(g):
        own[...] = part[sec, g].astype(F32)

        from_left, from_right = sec > 0, sec < n_sec - 1
        if g == shared:
            from_left = jnp.logical_and(from_left, sec != 1)
            from_right = jnp.logical_and(from_right, sec != n_sec - 2)

        @pl.when(from_left)
        def _():
            right_copy(sec, g).wait_recv()
            own[...] += rec_r[sec, g].astype(F32)

        @pl.when(from_right)
        def _():
            left_copy(sec, g).wait_recv()
            own[...] += rec_l[sec, g].astype(F32)

        key_out[:, g * HD : (g + 1) * HD] = own[0]
        value_out[:, g * HD : (g + 1) * HD] = own[1]

    unpack(0)
    beside = jnp.where(sec > 0, 1, 0) + jnp.where(sec < n_sec - 1, 1, 0)
    pl.semaphore_wait(barrier, n_key - 1 + n_head - 1 + beside)
    if shared >= 0:

        @pl.when(ends)
        def _():
            help_copy(0).start()
            help_copy(1).start()

    w_load.start()
    pass_one(0)
    for g in range(1, kvl):
        unpack(g)
    pass_two(0)
    if kvl > 1:
        pass_one(1)
    for g in range(1, kvl):
        if g + 1 < kvl:
            pass_one(g + 1)
        if g < kvl - 1:
            relay(g - 1)
        pass_two(g)
    if kvl > 1:
        relay(kvl - 2)
    if shared >= 0:
        pl.when(helpers)(assist)

    width = group * HD
    for g in range(kvl):
        for d in range(1, n_key):
            dq_copy(d, g).wait_recv()
        total = dqb[g, key].astype(F32)
        for d in range(1, n_key):
            total = total + dqr[d - 1, g].astype(F32)
        qlow[:, g * width : (g + 1) * width] = total.astype(BF16)
    w_load.wait()
    wide = w_v.shape[0]
    tile = 512

    def columns(i, carry):
        first = pl.multiple_of(i * tile, tile)
        product = dot(qlow[...], w_v[pl.ds(first, tile), :], NT).astype(BF16)
        for hh in range(n_head):
            pin[hh, :, pl.ds(first, tile)] = product[hh * block_out : (hh + 1) * block_out]
        return carry

    half = wide // tile // 2
    lax.fori_loop(0, half, columns, 0)
    relay(kvl - 1)
    lax.fori_loop(half, wide // tile, columns, 0)
    for d in range(1, n_head):
        in_copy(d).start()
    for stage in range(kvl, kvl + n_sec - 2):
        relay(stage)
    for g in range(kvl):
        finish(g)

    for d in range(1, n_head):
        in_copy(d).wait_recv()
    total = pin[head].astype(F32)
    for d in range(1, n_head):
        total = total + pin_r[d - 1].astype(F32)
    in_out[...] = total.astype(BF16)

    for g in range(kvl):
        for d in range(1, n_key):
            st_copy(d, g).wait_send()
            dq_copy(d, g).wait_send()

        def drain(c, carry, g=g):
            to_right, to_left = c > sec, c < sec
            if g == shared:
                to_right = jnp.logical_and(to_right, sec != 0)
                to_left = jnp.logical_and(to_left, sec != n_sec - 1)

            @pl.when(to_right)
            def _():
                right_copy(c, g).wait_send()

            @pl.when(to_left)
            def _():
                left_copy(c, g).wait_send()

            return carry

        lax.fori_loop(0, n_sec, drain, 0)
    for d in range(1, n_head):
        in_copy(d).wait_send()
    if shared >= 0:

        @pl.when(ends)
        def _():
            for i in range(3):
                help_copy(i).wait_send()


def hand_out(*refs):
    ins, outs, held, sem = refs[:3], refs[3:6], refs[6:9], refs[9]
    come = [pltpu.make_async_copy(ins[i], held[i], sem.at[0, i]) for i in range(3)]
    leave = [pltpu.make_async_copy(held[i], outs[i], sem.at[1, i]) for i in range(3)]
    for copy in come:
        copy.start()
    for i in range(3):
        come[i].wait()
        leave[i].start()
    for copy in leave:
        copy.wait()


def body(n_sec, n_head, n_key, queries, attn_grad, query_weight, kc, ke, vc, ve):
    rows, cols = queries.shape[1:]
    wide = query_weight.shape[1]
    positions, kv_cols = kc.shape
    kvl = kv_cols // HD
    group_rows = cols // kv_cols * rows
    rows_c = positions // n_sec
    block_out = rows // (n_head * n_key)
    group_cols = cols // kvl
    vmem = pltpu.VMEM
    dma = pltpu.SemaphoreType.DMA
    anywhere = pl.BlockSpec(memory_space=pl.ANY)
    in_vmem = pl.BlockSpec(memory_space=pltpu.VMEM)
    results = pl.pallas_call(
        functools.partial(kernel, n_sec, n_head, n_key),
        out_shape=(
            jax.ShapeDtypeStruct((block_out, wide), BF16),
            jax.ShapeDtypeStruct((rows_c, kv_cols), F32),
            jax.ShapeDtypeStruct((rows_c, kv_cols), F32),
        ),
        in_specs=[anywhere] * 7,
        out_specs=(in_vmem, in_vmem, in_vmem),
        scratch_shapes=[
            vmem(ke.T.shape, jnp.int32),
            vmem(ve.T.shape, jnp.int32),
            vmem((wide, cols), BF16),
            vmem((positions, kv_cols), jnp.int32),
            vmem((positions, kv_cols), jnp.int32),
            vmem((kvl, n_sec, rows_c, HD), BF16),
            vmem((kvl, n_sec, rows_c, HD), BF16),
            vmem((kvl, group_rows, HD), BF16),
            vmem((kvl, group_rows, HD), BF16),
            vmem((2, n_sec, rows_c, group_rows), F32),
            vmem((2, n_sec, rows_c, group_rows), F32),
            vmem((2, n_sec, 8, group_rows), F32),
            vmem((n_key, kvl, 8, group_rows), F32),
            vmem((HD, group_rows), F32),
            vmem((kvl, n_key, n_head * block_out, group_cols), BF16),
            vmem((n_key - 1, kvl, n_head * block_out, group_cols), BF16),
            vmem((n_head * block_out, cols), BF16),
            vmem((n_head, block_out, wide), BF16),
            vmem((n_head - 1, block_out, wide), BF16),
            vmem((n_sec, kvl, 2, rows_c, HD), BF16),
            vmem((n_sec, kvl, 2, rows_c, HD), BF16),
            vmem((n_sec, kvl, 2, rows_c, HD), BF16),
            vmem((2, rows_c, HD), F32),
            vmem((group_rows, HD), BF16),
            vmem((group_rows, HD), BF16),
            vmem((8, group_rows), F32),
            vmem((8, group_rows), F32),
            dma((2,)),
            dma((2, kvl)),
            dma((2, kvl, cols // kv_cols)),
            dma,
            dma((n_key, kvl)),
            dma((n_key, kvl)),
            dma((n_key, kvl)),
            dma((n_key, kvl)),
            dma((n_head,)),
            dma((n_head,)),
            dma((n_sec, kvl)),
            dma((n_sec, kvl)),
            dma((n_sec, kvl)),
            dma((3,)),
            dma((3,)),
        ],
        compiler_params=pltpu.CompilerParams(
            collective_id=0, has_side_effects=True, vmem_limit_bytes=58 * 1024 * 1024
        ),
    )(queries[0], attn_grad[0], query_weight[0], kc, ke.T, vc, ve.T)
    input_grad, key_grad, value_grad = pl.pallas_call(
        hand_out,
        out_shape=tuple(jax.ShapeDtypeStruct(r.shape, r.dtype) for r in results),
        in_specs=[anywhere] * 3,
        out_specs=(anywhere,) * 3,
        scratch_shapes=[vmem(r.shape, r.dtype) for r in results] + [dma((2, 3))],
        compiler_params=pltpu.CompilerParams(vmem_limit_bytes=62 * 1024 * 1024),
    )(*results)
    return input_grad[None], key_grad, value_grad


def solution(mesh):
    shape = mesh.shape
    return jax.shard_map(
        functools.partial(body, shape["section"], shape["head"], shape["key"]),
        mesh=mesh,
        in_specs=(
            P("section", None, "head"),
            P("section", None, "head"),
            P("section", None, "head"),
            P("key", "head"),
            P("key", "head"),
            P("key", "head"),
            P("key", "head"),
        ),
        out_specs=(
            P("section", ("head", "key"), None),
            P(("key", "section"), "head"),
            P(("key", "section"), "head"),
        ),
        check_vma=False,
    )
```
